256 devices in a mesh: grid: 64 (over y, x_hi, z), heads: 4 (over x_lo, core).
Axes of the slice: x: 4 (x_hi: 2, x_lo: 2; x = x_hi * 2 + x_lo), y: 4, z: 8, core: 2. Of those that a mesh axis runs over, the one named last changes fastest.
Arguments:
- tokens: bfloat16 [64, 8, 64, 1024], P('grid', None, None, 'heads'), may hold values from -16 to 16
- qkv_weight: bfloat16 [3, 1024, 1024], P(None, None, 'heads'), may hold values from -0.1875 to 0.1875
- out_weight: bfloat16 [1024, 1024], P('heads'), may hold values from -0.1875 to 0.1875
- out_grad: bfloat16 [64, 8, 64, 1024], P('grid', None, None, 'heads'), may hold values from -16 to 16
Outputs:
- d_tokens: bfloat16 [64, 8, 64, 1024], P('grid', None, None, 'heads')
- d_qkv_weight: float32 [3, 1024, 1024], P(None, 'grid', 'heads')
- d_out_weight: float32 [1024, 1024], P('heads', 'grid')
The draws below stay inside these ranges and needn't reach their ends.
All inputs are finite; a program needn't handle non-finite values.
Results may differ from the reference program's by a relative error of at most 0.023.
Values may be sent and summed in bfloat16 or wider, within the bound.
A program may use at most 128 MiB of HBM per device.

```python
import jax
import jax.numpy as jnp
from jax import lax

D = 1024
HEADS = 16
HD = 64
RADIUS = 6
LON_TILES = 8
TH = 8
TW = 64
LAT_TILES = 8
TILES = 64
NLAT = 64
NLON = 512


def with_spikes(drawn, stream_key, source, target, parts, factor):
    owner, partner = [(jnp.arange(drawn.shape[axis_at]) // (drawn.shape[axis_at] // parts)).reshape([-1 if axis == axis_at else 1 for axis in range(drawn.ndim)]) for axis_at in (source, target)]
    chosen = jax.random.permutation(stream_key, parts)[partner]
    strong = (owner == chosen) | (owner == (partner + parts // 2) % parts)
    return jnp.where(strong, factor * drawn, drawn)


def shard_levels(stream_key, dims, pieces, smallest, largest):
    def one(dim, shards_of):
        draws = jax.random.uniform(jax.random.fold_in(jax.random.fold_in(stream_key, 6), dim), (shards_of,), jnp.float32, smallest / len(pieces), largest / len(pieces))
        return jnp.repeat(jnp.exp(draws), dims[dim] // shards_of).reshape((-1,) + (1,) * (len(dims) - dim - 1))

    level = one(*pieces[0])
    for cut in pieces[1:]:
        level = level * one(*cut)
    return level


def bell_draw(rng, extent, scale, reach, pieces=(), kind=jnp.bfloat16):
    drawn = scale * jax.random.normal(rng, extent, jnp.float32)
    if pieces:
        drawn = drawn * shard_levels(rng, extent, pieces, -0.22, 0.18)
    return jnp.clip(drawn, -reach, reach).astype(kind)


def gaussian_with(rng, shape, width, most, split, heavy, held_as=jnp.bfloat16):
    entries = width * jax.random.normal(rng, shape, jnp.float32)
    if split:
        entries = entries * shard_levels(rng, shape, split, -0.22, 0.18)
    return jnp.clip(with_spikes(entries, jax.random.fold_in(rng, 3), *heavy), -most, most).astype(held_as)


def setup_inputs(seed: int = 0) -> dict:
    streams_of = jax.random.split(jax.random.key(seed), 5)
    return {
        "tokens": gaussian_with(streams_of[0], (TILES, TH, TW, D), 1.0, 16.0, ((0, 64), (3, 4)), (0, 3, 64, 4.0)),
        "qkv_weight": bell_draw(streams_of[1], (3, D, D), D ** -0.5, 0.1875, ((2, 4),)),
        "out_weight": bell_draw(streams_of[2], (D, D), D ** -0.5, 0.1875, ((0, 4),)),
        "out_grad": gaussian_with(streams_of[3], (TILES, TH, TW, D), 1.0, 16.0, ((0, 64), (3, 4)), (0, 3, 64, 4.0)),
    }


def to_field(tiles):
    feature_count = tiles.shape[-1]
    arranged = tiles.reshape(LON_TILES, LAT_TILES, TH, TW, feature_count)
    return arranged.transpose(1, 2, 0, 3, 4).reshape(NLAT, NLON, feature_count)


def to_tiles(field):
    feature_count = field.shape[-1]
    arranged = field.reshape(LAT_TILES, TH, LON_TILES, TW, feature_count)
    return arranged.transpose(2, 0, 1, 3, 4).reshape(TILES, TH, TW, feature_count)


def shifted(padded, shift_row, shift_col):
    rows_taken = lax.dynamic_slice_in_dim(padded, (shift_row + RADIUS).astype(jnp.int32), NLAT, 0)
    return jnp.roll(rows_taken, -shift_col, axis=1)


def placed(running, term, shift_row, shift_col):
    first_row = (shift_row + RADIUS).astype(jnp.int32)
    current = lax.dynamic_slice_in_dim(running, first_row, NLAT, 0)
    return lax.dynamic_update_slice_in_dim(running, current + jnp.roll(term, shift_col, axis=1), first_row, 0)


def per_head(values_in):
    return values_in.astype(jnp.float32).reshape(NLAT, NLON, HEADS, HD)


def reference(tokens, qkv_weight, out_weight, out_grad):
    kernel_side = 2 * RADIUS + 1
    offsets = jnp.arange(kernel_side * kernel_side, dtype=jnp.int32)
    rows_off = offsets // kernel_side - RADIUS
    cols_off = offsets % kernel_side - RADIUS
    score_scale = HD ** -0.5
    token_rows = to_field(tokens).reshape(NLAT * NLON, D)
    grad_rows = to_field(out_grad).reshape(NLAT * NLON, D)
    queries = jnp.dot(token_rows, qkv_weight[0], preferred_element_type=jnp.float32).astype(jnp.bfloat16)
    key_proj = jnp.dot(token_rows, qkv_weight[1], preferred_element_type=jnp.float32).astype(jnp.bfloat16)
    value_proj = jnp.dot(token_rows, qkv_weight[2], preferred_element_type=jnp.float32).astype(jnp.bfloat16)
    d_out = jnp.dot(grad_rows, out_weight.T, preferred_element_type=jnp.float32).astype(jnp.bfloat16)
    query_heads = per_head(queries)
    key_heads = per_head(key_proj)
    value_heads = per_head(value_proj)
    grad_heads = per_head(d_out)
    row_padding = ((RADIUS, RADIUS), (0, 0), (0, 0), (0, 0))
    key_padded = jnp.pad(key_heads, row_padding)
    value_padded = jnp.pad(value_heads, row_padding)
    row_valid = jnp.pad(jnp.ones((NLAT,), jnp.float32), RADIUS)

    def score_at(offset):
        return score_scale * jnp.sum(query_heads * shifted(key_padded, rows_off[offset], cols_off[offset]), -1)

    def valid_at(offset):
        return lax.dynamic_slice_in_dim(row_valid, (rows_off[offset] + RADIUS).astype(jnp.int32), NLAT, 0)

    scores = lax.map(score_at, offsets)
    key_valid = lax.map(valid_at, offsets)
    weights_raw = jnp.where(key_valid[:, :, None, None] > 0.5, jnp.exp(scores), 0.0)
    softmax = weights_raw / jnp.sum(weights_raw, axis=0)
    softmax_b = lax.optimization_barrier(softmax.astype(jnp.bfloat16)).astype(jnp.float32)

    def attend_step(offset, running):
        return running + softmax_b[offset][..., None] * shifted(value_padded, rows_off[offset], cols_off[offset])

    zero_heads = jnp.zeros((NLAT, NLON, HEADS, HD), jnp.float32)
    attended = lax.fori_loop(0, kernel_side * kernel_side, attend_step, zero_heads).astype(jnp.bfloat16)
    attended_rows = attended.reshape(NLAT * NLON, D)
    d_out_weight = jnp.dot(attended_rows.T, grad_rows, preferred_element_type=jnp.float32)
    row_delta = jnp.sum(grad_heads * attended.astype(jnp.float32), -1)

    def dprob_at(offset):
        return jnp.sum(grad_heads * shifted(value_padded, rows_off[offset], cols_off[offset]), -1)

    d_probs = lax.map(dprob_at, offsets)
    d_scores = softmax * (d_probs - row_delta[None])
    d_scores_b = lax.optimization_barrier(d_scores.astype(jnp.bfloat16)).astype(jnp.float32)

    def query_step(offset, running):
        return running + d_scores_b[offset][..., None] * shifted(key_padded, rows_off[offset], cols_off[offset])

    d_query = score_scale * lax.fori_loop(0, kernel_side * kernel_side, query_step, zero_heads)

    def key_step(offset, carried):
        key_acc, value_acc = carried
        key_acc = placed(key_acc, d_scores_b[offset][..., None] * query_heads, rows_off[offset], cols_off[offset])
        value_acc = placed(value_acc, softmax_b[offset][..., None] * grad_heads, rows_off[offset], cols_off[offset])
        return key_acc, value_acc

    zero_padded = jnp.zeros((NLAT + 2 * RADIUS, NLON, HEADS, HD), jnp.float32)
    key_acc, value_acc = lax.fori_loop(0, kernel_side * kernel_side, key_step, (zero_padded, zero_padded))
    d_key = score_scale * key_acc[RADIUS:RADIUS + NLAT]
    d_value = value_acc[RADIUS:RADIUS + NLAT]
    gradients = [part.reshape(NLAT * NLON, D).astype(jnp.bfloat16) for part in (d_query, d_key, d_value)]
    d_qkv_weight = jnp.stack([jnp.dot(token_rows.T, part, preferred_element_type=jnp.float32) for part in gradients])
    d_input = jnp.dot(gradients[0], qkv_weight[0].T, preferred_element_type=jnp.float32)
    d_input = d_input + jnp.dot(gradients[1], qkv_weight[1].T, preferred_element_type=jnp.float32)
    d_input = d_input + jnp.dot(gradients[2], qkv_weight[2].T, preferred_element_type=jnp.float32)
    d_tokens = to_tiles(d_input.astype(jnp.bfloat16).reshape(NLAT, NLON, D))
    return d_tokens, d_qkv_weight, d_out_weight
```

```python
import jax
import jax.numpy as jnp
from jax import lax
from jax.experimental import pallas as pl
from jax.experimental.pallas import tpu as pltpu
from jax.sharding import PartitionSpec as P

MESH = pl.DeviceIdType.MESH
F32 = jnp.float32
BF16 = jnp.bfloat16

HD = 64
RAD = 6
LON = 8
LAT = 8
TH = 8
TW = 64
WID = 256
ROWS = TH * TW
EXT_R = TH + 2 * RAD
PAD = 8
EXT_C = TW + 2 * PAD
BW = 16
WINC = BW + 2 * PAD
KEYS = EXT_R * WINC
QN = TH * BW
SLAB = RAD * TW
EDGE = TH * PAD
CORNER = RAD * PAD

WAYS = ((-1, 0), (1, 0), (0, -1), (0, 1), (-1, -1), (-1, 1), (1, -1), (1, 1))


def mm(a, b, ca=1, cb=0):
    return lax.dot_general(a, b, (((ca,), (cb,)), ((), ())), preferred_element_type=F32)


def kernel(
    x_ref, g_ref, w_any, wo_any,
    tok_ref, eo_ref, lo_ref,
    w_v, wo_v, xf, gf, acc, kvb, edge, ns_r, ew_r, dg_r, kvx, gx,
    q_s, do_s, o_s, dq_s, dkv, bias, xt, gt,
    gns_s, gew_s, gdg_s, gns_r, gew_r, gdg_r,
    e_s, e_r, l_s, l_r, own_e, own_l, pe_b, pl_b, e2_r, l2_r,
    tacc, t_s, t_r,
    w_sem, ag_ss, ag_rs, h_ss, h_rs, b_ss, b_rs,
    e_ss, e_rs, l_ss, l_rs, e2_ss, e2_rs, l2_ss, l2_rs, t_ss, t_rs,
):
    g = lax.axis_index("grid")
    h = lax.axis_index("heads")
    lat = lax.rem(g, LAT)
    lon = lax.div(g, LAT)
    sib = h + 1 - 2 * lax.rem(h, 2)
    far = h + 2 - 4 * lax.div(h, 2)
    opp = 3 - h
    slots = (h, sib, far, opp)

    w_copy = pltpu.make_async_copy(w_any, w_v, w_sem.at[0])
    wo_copy = pltpu.make_async_copy(wo_any, wo_v, w_sem.at[1])
    w_copy.start()
    wo_copy.start()

    def tile(dlat, dlon):
        return lax.rem(lon + dlon + LON, LON) * LAT + lax.rem(lat + dlat + LAT, LAT)

    def can_send(way):
        dlat = WAYS[way][0]
        return (lat + dlat >= 0) & (lat + dlat < LAT)

    def can_recv(way):
        dlat = WAYS[way][0]
        return (lat - dlat >= 0) & (lat - dlat < LAT)

    def when(cond_way, way, fn):
        if WAYS[way][0] == 0:
            fn()
        else:
            pl.when(cond_way(way))(fn)

    bar = pltpu.get_barrier_semaphore()

    def greet(to_grid, to_head):
        pl.semaphore_signal(bar, inc=1, device_id=(to_grid, to_head), device_id_type=MESH)

    greet(g, sib)
    greet(g, far)
    for k in range(1, 8):
        greet(tile(k, 0), h)
        greet(tile(0, k), h)
    for way in range(4, 8):
        when(can_send, way, lambda way=way: greet(tile(*WAYS[way]), h))
    has_n = (lat > 0).astype(jnp.int32)
    has_s = (lat < LAT - 1).astype(jnp.int32)
    pl.semaphore_wait(bar, 16 + 2 * has_n + 2 * has_s)

    def rcopy(src, dst, ss, rs, to_grid, to_head):
        return pltpu.make_async_remote_copy(
            src_ref=src, dst_ref=dst, send_sem=ss, recv_sem=rs,
            device_id=(to_grid, to_head), device_id_type=MESH,
        )

    def gather(src, full, base):
        return (
            rcopy(src, full.at[0], ag_ss.at[base], ag_rs.at[base], g, sib),
            rcopy(src, full.at[1], ag_ss.at[base + 1], ag_rs.at[base + 1], g, far),
            rcopy(full.at[1], full.at[2], ag_ss.at[base + 2], ag_rs.at[base + 2], g, sib),
        )

    x_sib, x_far, x_fwd = gather(x_ref, xf, 0)
    g_sib, g_far, g_fwd = gather(g_ref, gf, 3)
    x_far.start()
    x_sib.start()
    w_copy.wait()

    def add_kv(block, k):
        for c in range(2):
            part = mm(block, w_v[c + 1, slots[k]])
            cols = slice(c * WID, (c + 1) * WID)
            acc[:, cols] = part if k == 0 else acc[:, cols] + part

    add_kv(x_ref[...], 0)
    x_sib.wait_recv()
    add_kv(xf[0], 1)
    x_far.wait_recv()
    x_fwd.start()
    g_far.start()
    g_sib.start()
    add_kv(xf[1], 2)
    x_fwd.wait_recv()
    add_kv(xf[2], 3)

    def round_kv(i, carry):
        rows = pl.ds(pl.multiple_of(i * TW, TW), TW)
        value = acc[rows, :].astype(BF16)
        kvb[rows, :] = value
        kvx[i + RAD, PAD : PAD + TW, :] = value.astype(F32)
        return carry

    lax.fori_loop(0, TH, round_kv, 0)

    def halo_copy(way, srcs, dsts, ss, rs):
        dlat, dlon = WAYS[way]
        return rcopy(srcs[way], dsts[way], ss.at[way], rs.at[way], tile(dlat, dlon), h)

    halo_dst = [ns_r.at[0], ns_r.at[1], ew_r.at[0], ew_r.at[1]] + [dg_r.at[i] for i in range(4)]
    halo_src = [
        kvb.at[0:SLAB],
        kvb.at[ROWS - SLAB : ROWS],
        edge.at[0],
        edge.at[1],
        edge.at[0, 0:CORNER],
        edge.at[1, 0:CORNER],
        edge.at[0, EDGE - CORNER : EDGE],
        edge.at[1, EDGE - CORNER : EDGE],
    ]
    halo = [halo_copy(way, halo_src, halo_dst, h_ss, h_rs) for way in range(8)]
    for way in range(2):
        when(can_send, way, halo[way].start)
    body = slice(RAD, RAD + TH)
    edge[0] = kvx[body, PAD : 2 * PAD, :].reshape(EDGE, 2 * WID).astype(BF16)
    edge[1] = kvx[body, TW : TW + PAD, :].reshape(EDGE, 2 * WID).astype(BF16)
    for way in range(2, 8):
        when(can_send, way, halo[way].start)

    x_blocks = (x_ref, xf.at[0], xf.at[1], xf.at[2])
    g_blocks = (g_ref, gf.at[0], gf.at[1], gf.at[2])
    left = acc.at[:, 0:WID]
    for k in range(4):
        part = mm(x_blocks[k][...], w_v[0, slots[k]])
        left[...] = part if k == 0 else left[...] + part
    q_s[...] = (left[...].astype(BF16) * jnp.asarray(HD**-0.5, BF16)).reshape(TH, TW, WID)

    def turn(blocks, out):
        for k in range(4):
            for j in range(2):
                piece = blocks[k][:, j * 128 : (j + 1) * 128].astype(F32)
                out[2 * slots[k] + j] = piece.T.astype(BF16)

    g_sib.wait_recv()
    g_far.wait_recv()
    g_fwd.start()
    turn(x_blocks, xt)

    key = lax.broadcasted_iota(jnp.int32, (KEYS, QN), 0)
    qry = lax.broadcasted_iota(jnp.int32, (KEYS, QN), 1)
    key_r, key_c = lax.div(key, WINC), lax.rem(key, WINC)
    dr = key_r - lax.div(qry, BW)
    dc = key_c - lax.rem(qry, BW)
    at_lat = key_r + (lat * TH - RAD)
    fine = (dr >= 0) & (dr <= 2 * RAD) & (dc >= PAD - RAD) & (dc <= PAD + RAD)
    fine = fine & (at_lat >= 0) & (at_lat < LAT * TH)
    bias[...] = jnp.where(fine, 0.0, -1e30)

    def clear(i, carry):
        gx[i] = jnp.zeros((EXT_C, 2 * WID), F32)
        return carry

    lax.fori_loop(0, EXT_R, clear, 0)

    wo_copy.wait()
    g_fwd.wait_recv()
    for k in range(4):
        cols = pl.ds(pl.multiple_of(slots[k] * WID, WID), WID)
        part = mm(g_blocks[k][...], wo_v[:, cols], 1, 1)
        left[...] = part if k == 0 else left[...] + part
    do_s[...] = left[...].astype(BF16).reshape(TH, TW, WID)
    turn(g_blocks, gt)

    def ext_at(way):
        dlat, dlon = WAYS[way]
        rows = {-1: slice(RAD + TH, EXT_R), 1: slice(0, RAD), 0: body}[dlat]
        cols = {-1: slice(PAD + TW, EXT_C), 1: slice(0, PAD), 0: slice(PAD, PAD + TW)}[dlon]
        return rows, cols

    def shape_of(rows, cols):
        return rows.stop - rows.start, cols.stop - cols.start, 2 * WID

    for way in range(8):
        rows, cols = ext_at(way)
        shape = shape_of(rows, cols)

        def take(way=way, rows=rows, cols=cols, shape=shape):
            halo[way].wait_recv()
            kvx[rows, cols, :] = halo_dst[way][...].astype(F32).reshape(shape)

        def blank(rows=rows, cols=cols, shape=shape):
            kvx[rows, cols, :] = jnp.zeros(shape, F32)

        when(can_recv, way, take)
        if WAYS[way][0] != 0:
            pl.when(jnp.logical_not(can_recv(way)))(blank)

    lane = lax.broadcasted_iota(jnp.int32, (QN, 128), 1)
    first = lane < HD

    def two_heads(value):
        zero = jnp.zeros_like(value)
        return jnp.concatenate([jnp.where(first, value, zero), jnp.where(first, zero, value)], axis=0)

    def untwo(value):
        picked = jnp.concatenate([value[:HD, :QN], value[HD:, QN:]], axis=0)
        return picked.T.astype(BF16).reshape(TH, BW, 128)

    def block(b, carry):
        start = pl.multiple_of(b * BW, BW)
        mine = pl.ds(start, BW)
        window = pl.ds(start, WINC)
        for p in range(2):
            cols = slice(p * 128, (p + 1) * 128)
            vcols = slice(WID + p * 128, WID + (p + 1) * 128)
            keys = kvx[:, window, cols].reshape(KEYS, 128).astype(BF16)
            vals = kvx[:, window, vcols].reshape(KEYS, 128).astype(BF16)
            qq = two_heads(q_s[:, mine, cols].reshape(QN, 128))
            dd = two_heads(do_s[:, mine, cols].reshape(QN, 128))
            scores = mm(keys, qq, 1, 1)
            b1 = bias[...]
            raw = jnp.exp(scores + jnp.concatenate([b1, b1], axis=1))
            prob = raw * (1.0 / jnp.sum(raw, axis=0, keepdims=True))
            prob_b = prob.astype(BF16)
            d_prob = mm(vals, dd, 1, 1)
            delta = jnp.sum(prob * d_prob, axis=0, keepdims=True)
            d_sc = (prob * (d_prob - delta)).astype(BF16)
            o_s[:, mine, cols] = untwo(mm(vals, prob_b, 0, 0))
            dq_s[:, mine, cols] = untwo(mm(keys, d_sc, 0, 0) * HD**-0.5)
            gx[:, window, cols] += mm(d_sc, qq).reshape(EXT_R, WINC, 128)
            gx[:, window, vcols] += mm(prob_b, dd).reshape(EXT_R, WINC, 128)
        return carry

    lax.fori_loop(0, TW // BW, block, 0)

    back_src = [gns_s.at[0], gns_s.at[1], gew_s.at[0], gew_s.at[1]] + [gdg_s.at[i] for i in range(4)]
    back_dst = [gns_r.at[0], gns_r.at[1], gew_r.at[0], gew_r.at[1]] + [gdg_r.at[i] for i in range(4)]
    back = [halo_copy(way, back_src, back_dst, b_ss, b_rs) for way in range(8)]
    for way in range(8):
        dlat, dlon = WAYS[way]
        rows = {-1: slice(0, RAD), 1: slice(RAD + TH, EXT_R), 0: body}[dlat]
        cols = {-1: slice(0, PAD), 1: slice(PAD + TW, EXT_C), 0: slice(PAD, PAD + TW)}[dlon]
        flat = (rows.stop - rows.start) * (cols.stop - cols.start)

        def give(way=way, rows=rows, cols=cols, flat=flat):
            back_src[way][...] = gx[rows, cols, :].reshape(flat, 2 * WID).astype(BF16)
            back[way].start()

        when(can_send, way, give)

    def e_chunk(chunk):
        dq = dq_s[...].reshape(ROWS, WID)
        oo = o_s[...].reshape(ROWS, WID)
        return jnp.concatenate([mm(xt[chunk], dq), mm(gt[chunk], oo)], axis=1)

    def e_copy(k):
        return rcopy(e_s.at[k], e_r.at[k], e_ss.at[k], e_rs.at[k], tile(0, k + 1), h)

    def l_copy(k):
        return rcopy(l_s.at[k], l_r.at[k], l_ss.at[k], l_rs.at[k], tile(0, k + 1), h)

    def e_step(k, carry):
        e_s[k] = e_chunk(lax.rem(lon + k + 1, LON)).astype(BF16)
        e_copy(k).start()
        return carry

    lax.fori_loop(0, LON - 1, e_step, 0)
    own_e[...] = e_chunk(lon)

    for s in range(4):
        tacc[s] = mm(dq_s[...].reshape(ROWS, WID), w_v[0, s], 1, 1)

    for way in range(8):
        dlat, dlon = WAYS[way]
        rows = {-1: slice(TH, RAD + TH), 1: slice(RAD, 2 * RAD), 0: body}[dlat]
        cols = {-1: slice(TW, TW + PAD), 1: slice(PAD, 2 * PAD), 0: slice(PAD, PAD + TW)}[dlon]
        shape = shape_of(rows, cols)

        def fold(way=way, rows=rows, cols=cols, shape=shape):
            back[way].wait_recv()
            gx[rows, cols, :] += back_dst[way][...].astype(F32).reshape(shape)

        when(can_recv, way, fold)

    def round_g(i, carry):
        rows = pl.ds(pl.multiple_of(i * TW, TW), TW)
        dkv[rows, :] = gx[i + RAD, PAD : PAD + TW, :].astype(BF16)
        return carry

    lax.fori_loop(0, TH, round_g, 0)

    def l_step(k, carry):
        l_s[k] = mm(xt[lax.rem(lon + k + 1, LON)], dkv[...]).astype(BF16)
        l_copy(k).start()
        return carry

    lax.fori_loop(0, LON - 1, l_step, 0)
    own_l[...] = mm(xt[lon], dkv[...])

    def t_full(s):
        return (
            tacc[s]
            + mm(dkv[:, 0:WID], w_v[1, s], 1, 1)
            + mm(dkv[:, WID : 2 * WID], w_v[2, s], 1, 1)
        )

    t_opp = rcopy(t_s.at[0], t_r.at[0], t_ss.at[0], t_rs.at[0], g, sib)
    t_sib = rcopy(t_s.at[1], t_r.at[1], t_ss.at[1], t_rs.at[1], g, sib)
    t_far = rcopy(t_s.at[2], t_r.at[2], t_ss.at[2], t_rs.at[2], g, far)
    t_s[0] = t_full(opp).astype(BF16)
    t_opp.start()
    t_s[1] = t_full(sib).astype(BF16)
    t_sib.start()
    far_part = t_full(far)
    t_opp.wait_recv()
    t_s[2] = (far_part + t_r[0].astype(F32)).astype(BF16)
    t_far.start()
    tacc[h] = t_full(h)

    def e2_copy(k):
        to = lax.rem(lat + k + 1, LAT)
        rows = pl.ds(pl.multiple_of(to * 16, 16), 16)
        return rcopy(pe_b.at[rows], e2_r.at[k], e2_ss.at[k], e2_rs.at[k], tile(k + 1, 0), h)

    def l2_copy(k):
        to = lax.rem(lat + k + 1, LAT)
        rows = pl.ds(pl.multiple_of(to * 16, 16), 16)
        return rcopy(pl_b.at[rows], l2_r.at[k], l2_ss.at[k], l2_rs.at[k], tile(k + 1, 0), h)

    def level(own, first_copy, recv, packed, second_copy):
        def add(k, carry):
            first_copy(k).wait_recv()
            own[...] += recv[k].astype(F32)
            return carry

        lax.fori_loop(0, LON - 1, add, 0)
        packed[...] = own[...].astype(BF16)

        def send(k, carry):
            second_copy(k).start()
            return carry

        lax.fori_loop(0, LAT - 1, send, 0)

    level(own_e, e_copy, e_r, pe_b, e2_copy)
    level(own_l, l_copy, l_r, pl_b, l2_copy)

    t_sib.wait_recv()
    t_far.wait_recv()
    tok_ref[...] = (tacc[h] + t_r[1].astype(F32) + t_r[2].astype(F32)).astype(BF16)

    def finish(out, own, second_copy, recv):
        out[...] = own[pl.ds(pl.multiple_of(lat * 16, 16), 16), :]

        def add(k, carry):
            second_copy(k).wait_recv()
            out[...] += recv[k].astype(F32)
            return carry

        lax.fori_loop(0, LAT - 1, add, 0)

    finish(eo_ref, own_e, e2_copy, e2_r)
    finish(lo_ref, own_l, l2_copy, l2_r)

    for copy in (x_sib, x_far, x_fwd, g_sib, g_far, g_fwd, t_opp, t_sib, t_far):
        copy.wait_send()
    for way in range(8):
        when(can_send, way, halo[way].wait_send)
        when(can_send, way, back[way].wait_send)

    def drain(k, carry):
        e_copy(k).wait_send()
        l_copy(k).wait_send()
        e2_copy(k).wait_send()
        l2_copy(k).wait_send()
        return carry

    lax.fori_loop(0, LON - 1, drain, 0)


def local(tokens, qkv_weight, out_weight, out_grad):
    vm = pltpu.VMEM
    dma = pltpu.SemaphoreType.DMA
    scratch = [
        vm((3, 4, WID, WID), BF16),
        vm((WID, 4 * WID), BF16),
        vm((3, ROWS, WID), BF16),
        vm((3, ROWS, WID), BF16),
        vm((ROWS, 2 * WID), F32),
        vm((ROWS, 2 * WID), BF16),
        vm((2, EDGE, 2 * WID), BF16),
        vm((2, SLAB, 2 * WID), BF16),
        vm((2, EDGE, 2 * WID), BF16),
        vm((4, CORNER, 2 * WID), BF16),
        vm((EXT_R, EXT_C, 2 * WID), F32),
        vm((EXT_R, EXT_C, 2 * WID), F32),
        vm((TH, TW, WID), BF16),
        vm((TH, TW, WID), BF16),
        vm((TH, TW, WID), BF16),
        vm((TH, TW, WID), BF16),
        vm((ROWS, 2 * WID), BF16),
        vm((KEYS, QN), F32),
        vm((LON, 128, ROWS), BF16),
        vm((LON, 128, ROWS), BF16),
        vm((2, SLAB, 2 * WID), BF16),
        vm((2, EDGE, 2 * WID), BF16),
        vm((4, CORNER, 2 * WID), BF16),
        vm((2, SLAB, 2 * WID), BF16),
        vm((2, EDGE, 2 * WID), BF16),
        vm((4, CORNER, 2 * WID), BF16),
        vm((LON - 1, 128, 2 * WID), BF16),
        vm((LON - 1, 128, 2 * WID), BF16),
        vm((LON - 1, 128, 2 * WID), BF16),
        vm((LON - 1, 128, 2 * WID), BF16),
        vm((128, 2 * WID), F32),
        vm((128, 2 * WID), F32),
        vm((128, 2 * WID), BF16),
        vm((128, 2 * WID), BF16),
        vm((LAT - 1, 16, 2 * WID), BF16),
        vm((LAT - 1, 16, 2 * WID), BF16),
        vm((4, ROWS, WID), F32),
        vm((3, ROWS, WID), BF16),
        vm((3, ROWS, WID), BF16),
        dma((2,)),
        dma((6,)), dma((6,)),
        dma((8,)), dma((8,)),
        dma((8,)), dma((8,)),
        dma((7,)), dma((7,)),
        dma((7,)), dma((7,)),
        dma((7,)), dma((7,)),
        dma((7,)), dma((7,)),
        dma((3,)), dma((3,)),
    ]
    in_vmem = pl.BlockSpec(memory_space=pltpu.VMEM)
    anywhere = pl.BlockSpec(memory_space=pl.ANY)
    d_tok, early, late = pl.pallas_call(
        kernel,
        out_shape=(
            jax.ShapeDtypeStruct((ROWS, WID), BF16),
            jax.ShapeDtypeStruct((16, 2 * WID), F32),
            jax.ShapeDtypeStruct((16, 2 * WID), F32),
        ),
        in_specs=[in_vmem, in_vmem, anywhere, anywhere],
        out_specs=(in_vmem, in_vmem, in_vmem),
        scratch_shapes=scratch,
        compiler_params=pltpu.CompilerParams(
            collective_id=0, has_side_effects=True, vmem_limit_bytes=56 * 1024 * 1024
        ),
        cost_estimate=pl.CostEstimate(flops=8_000_000_000, bytes_accessed=4_000_000, transcendentals=1_400_000),
    )(
        tokens.reshape(ROWS, WID),
        out_grad.reshape(ROWS, WID),
        qkv_weight.reshape(3, 4, WID, WID),
        out_weight,
    )
    d_qkv = jnp.stack([early[:, :WID], late[:, :WID], late[:, WID:]])
    return d_tok.reshape(tokens.shape), d_qkv, early[:, WID:].T


def solution(mesh):
    in_specs = (
        P("grid", None, None, "heads"),
        P(None, None, "heads"),
        P("heads", None),
        P("grid", None, None, "heads"),
    )
    out_specs = (P("grid", None, None, "heads"), P(None, "grid", "heads"), P("heads", "grid"))
    return jax.shard_map(local, mesh=mesh, in_specs=in_specs, out_specs=out_specs, check_vma=False)
```

```python
import jax
import jax.numpy as jnp
from jax import lax
from jax.experimental import pallas as pl
from jax.experimental.pallas import tpu as pltpu
from jax.sharding import PartitionSpec as P

MESH = pl.DeviceIdType.MESH
F32 = jnp.float32
BF16 = jnp.bfloat16

HD = 64
RAD = 6
LON = 8
LAT = 8
TH = 8
TW = 64
WID = 256
ROWS = TH * TW
EXT_R = TH + 2 * RAD
PAD = 8
EXT_C = TW + 2 * PAD
BW = 16
WINC = BW + 2 * PAD
KEYS = EXT_R * WINC
QN = TH * BW
NB = TW // BW
SLAB = RAD * BW
EDGE = TH * PAD
CORNER = RAD * PAD
PIECES = EXT_C // BW
ORDER = (0, 3, 1, 2)


def mm(a, b, ca=1, cb=0):
    return lax.dot_general(a, b, (((ca,), (cb,)), ((), ())), preferred_element_type=F32)


def kernel(
    x_ref, g_ref, w_any, wo_any,
    tok_ref, eo_ref, lo_ref,
    w_v, wo_v, xf, gf, kvb, edge, ns_r, ew_r, co_r, kvx, gx,
    q_s, do_s, o_s, dq_s, dkv, bias, xt, gt,
    gns_s, gew_s, gns_r, gew_r,
    e_s, e_r, l_s, l_r, own_e, own_l, pe_b, pl_b, e2_r, l2_r,
    tacc, t_s, t_r,
    w_sem, x_ss, x_rs, g_ss, g_rs, n_ss, n_rs, s_ss, s_rs, ew_ss, ew_rs, co_ss, co_rs,
    bn_ss, bn_rs, bs_ss, bs_rs, be_ss, be_rs,
    e_ss, e_rs, l_ss, l_rs, e2_ss, e2_rs, l2_ss, l2_rs, t_ss, t_rs,
):
    g = lax.axis_index("grid")
    h = lax.axis_index("heads")
    lat = lax.rem(g, LAT)
    lon = lax.div(g, LAT)
    sib = h + 1 - 2 * lax.rem(h, 2)
    far = h + 2 - 4 * lax.div(h, 2)
    opp = 3 - h
    slots = (h, sib, far, opp)

    w_copy = pltpu.make_async_copy(w_any, w_v, w_sem.at[0])
    wo_copy = pltpu.make_async_copy(wo_any, wo_v, w_sem.at[1])
    w_copy.start()
    wo_copy.start()

    def tile(dlat, dlon):
        return lax.rem(lon + dlon + LON, LON) * LAT + lax.rem(lat + dlat + LAT, LAT)

    has_n = lat > 0
    has_s = lat < LAT - 1
    can_send = (has_n, has_s)
    can_recv = (has_s, has_n)
    step = (-1, 1)

    bar = pltpu.get_barrier_semaphore()

    def greet(to_grid, to_head):
        pl.semaphore_signal(bar, inc=1, device_id=(to_grid, to_head), device_id_type=MESH)

    greet(g, sib)
    greet(g, far)
    for k in range(1, 8):
        greet(tile(k, 0), h)
        greet(tile(0, k), h)
    pl.semaphore_wait(bar, 16)

    def rcopy(src, dst, ss, rs, to_grid, to_head):
        return pltpu.make_async_remote_copy(
            src_ref=src, dst_ref=dst, send_sem=ss, recv_sem=rs,
            device_id=(to_grid, to_head), device_id_type=MESH,
        )

    def gather(src, full, ss, rs, c):
        mine = src.at[:, c * BW : (c + 1) * BW, :]
        return (
            rcopy(mine, full.at[0, c], ss.at[c], rs.at[c], g, sib),
            rcopy(mine, full.at[1, c], ss.at[NB + c], rs.at[NB + c], g, far),
            rcopy(full.at[1, c], full.at[2, c], ss.at[2 * NB + c], rs.at[2 * NB + c], g, sib),
        )

    x_copies = [gather(x_ref, xf, x_ss, x_rs, c) for c in range(NB)]
    g_copies = [gather(g_ref, gf, g_ss, g_rs, c) for c in range(NB)]
    for c in ORDER:
        x_copies[c][1].start()
        x_copies[c][0].start()

    def chunk_of(ref, full, k, c):
        value = ref[:, c * BW : (c + 1) * BW, :] if k == 0 else full[k - 1, c]
        return value.reshape(QN, WID)

    key = lax.broadcasted_iota(jnp.int32, (KEYS, QN), 0)
    qry = lax.broadcasted_iota(jnp.int32, (KEYS, QN), 1)
    key_r, key_c = lax.div(key, WINC), lax.rem(key, WINC)
    dr = key_r - lax.div(qry, BW)
    dc = key_c - lax.rem(qry, BW)
    at_lat = key_r + (lat * TH - RAD)
    fine = (dr >= 0) & (dr <= 2 * RAD) & (dc >= PAD - RAD) & (dc <= PAD + RAD)
    fine = fine & (at_lat >= 0) & (at_lat < LAT * TH)
    bias[...] = jnp.where(fine, 0.0, -1e30)

    def clear(i, carry):
        gx[i] = jnp.zeros((EXT_C, 2 * WID), F32)
        return carry

    lax.fori_loop(0, EXT_R, clear, 0)
    body = slice(RAD, RAD + TH)
    rim = (slice(RAD + TH, EXT_R), slice(0, RAD))
    for way in range(2):

        def blank(way=way):
            kvx[rim[way], :, :] = jnp.zeros((RAD, EXT_C, 2 * WID), F32)

        pl.when(jnp.logical_not(can_recv[way]))(blank)
    w_copy.wait()

    def ns_copy(way, c):
        rows = slice(0, SLAB) if way == 0 else slice(QN - SLAB, QN)
        ss, rs = (n_ss, n_rs) if way == 0 else (s_ss, s_rs)
        return rcopy(kvb.at[c, rows], ns_r.at[way, c], ss.at[c], rs.at[c], tile(step[way], 0), h)

    def ew_copy(way):
        return rcopy(edge.at[way], ew_r.at[way], ew_ss.at[way], ew_rs.at[way], tile(0, step[way]), h)

    def corner_copy(way, side):
        rows = slice(0, CORNER) if way == 0 else slice(EDGE - CORNER, EDGE)
        at = 2 * way + side
        return rcopy(ew_r.at[side, rows], co_r.at[at], co_ss.at[at], co_rs.at[at], tile(step[way], 0), h)

    for c in ORDER:
        total = [None, None]

        def add_kv(k, c=c, total=total):
            block = chunk_of(x_ref, xf, k, c)
            for i in range(2):
                part = mm(block, w_v[i + 1, slots[k]])
                total[i] = part if total[i] is None else total[i] + part

        add_kv(0)
        x_copies[c][0].wait_recv()
        add_kv(1)
        x_copies[c][1].wait_recv()
        x_copies[c][2].start()
        if c == ORDER[-1]:
            for other in ORDER:
                g_copies[other][1].start()
                g_copies[other][0].start()
        add_kv(2)
        x_copies[c][2].wait_recv()
        add_kv(3)
        value = jnp.concatenate([total[0].astype(BF16), total[1].astype(BF16)], axis=1)
        kvb[c] = value
        for way in range(2):
            pl.when(can_send[way])(ns_copy(way, c).start)
        wide = value.astype(F32).reshape(TH, BW, 2 * WID)
        kvx[body, PAD + c * BW : PAD + (c + 1) * BW, :] = wide
        if c == 0:
            edge[0] = wide[:, :PAD, :].reshape(EDGE, 2 * WID).astype(BF16)
            ew_copy(0).start()
        if c == NB - 1:
            edge[1] = wide[:, BW - PAD :, :].reshape(EDGE, 2 * WID).astype(BF16)
            ew_copy(1).start()

    def turn(ref, full, out, c):
        for k in range(4):
            piece = chunk_of(ref, full, k, c)
            for j in range(2):
                part = piece[:, j * 128 : (j + 1) * 128].astype(F32)
                out[2 * slots[k] + j, :, c * QN : (c + 1) * QN] = part.T.astype(BF16)

    def query(c):
        total = mm(chunk_of(x_ref, xf, 0, c), w_v[0, slots[0]])
        for k in range(1, 4):
            total += mm(chunk_of(x_ref, xf, k, c), w_v[0, slots[k]])
        q_s[c] = total.astype(BF16) * jnp.asarray(HD**-0.5, BF16)

    for c in ORDER[:2]:
        query(c)
    for side in range(2):
        ew_copy(side).wait_recv()
        for way in range(2):
            pl.when(can_send[way])(corner_copy(way, side).start)
    for c in ORDER[2:]:
        query(c)
    for c in range(NB):
        turn(x_ref, xf, xt, c)
    for side in range(2):
        cols = slice(PAD + TW, EXT_C) if side == 0 else slice(0, PAD)
        kvx[body, cols, :] = ew_r[side].astype(F32).reshape(TH, PAD, 2 * WID)

    wo_copy.wait()
    for c in ORDER:
        g_copies[c][0].wait_recv()
        g_copies[c][1].wait_recv()
        g_copies[c][2].start()
        total = None
        for k in range(4):
            if k == 3:
                g_copies[c][2].wait_recv()
            cols = pl.ds(pl.multiple_of(slots[k] * WID, WID), WID)
            part = mm(chunk_of(g_ref, gf, k, c), wo_v[:, cols], 1, 1)
            total = part if total is None else total + part
        do_s[c] = total.astype(BF16)
        turn(g_ref, gf, gt, c)

    def take_chunk(c):
        for way in range(2):

            def take(way=way):
                ns_copy(way, c).wait_recv()
                value = ns_r[way, c].astype(F32).reshape(RAD, BW, 2 * WID)
                kvx[rim[way], PAD + c * BW : PAD + (c + 1) * BW, :] = value

            pl.when(can_recv[way])(take)

    def take_corners(side):
        cols = slice(PAD + TW, EXT_C) if side == 0 else slice(0, PAD)
        for way in range(2):

            def take(way=way):
                corner_copy(way, side).wait_recv()
                kvx[rim[way], cols, :] = co_r[2 * way + side].astype(F32).reshape(RAD, PAD, 2 * WID)

            pl.when(can_recv[way])(take)

    lane = lax.broadcasted_iota(jnp.int32, (QN, 128), 1)
    first = lane < HD

    def two_heads(value):
        zero = jnp.zeros_like(value)
        return jnp.concatenate([jnp.where(first, value, zero), jnp.where(first, zero, value)], axis=0)

    def untwo(value):
        picked = jnp.concatenate([value[:HD, :QN], value[HD:, QN:]], axis=0)
        return picked.T.astype(BF16)

    def block(b):
        window = slice(b * BW, b * BW + WINC)
        for p in range(2):
            cols = slice(p * 128, (p + 1) * 128)
            vcols = slice(WID + p * 128, WID + (p + 1) * 128)
            keys = kvx[:, window, cols].reshape(KEYS, 128).astype(BF16)
            vals = kvx[:, window, vcols].reshape(KEYS, 128).astype(BF16)
            qq = two_heads(q_s[b, :, cols])
            dd = two_heads(do_s[b, :, cols])
            scores = mm(keys, qq, 1, 1)
            b1 = bias[...]
            raw = jnp.exp(scores + jnp.concatenate([b1, b1], axis=1))
            prob = raw * (1.0 / jnp.sum(raw, axis=0, keepdims=True))
            prob_b = prob.astype(BF16)
            d_prob = mm(vals, dd, 1, 1)
            delta = jnp.sum(prob * d_prob, axis=0, keepdims=True)
            d_sc = (prob * (d_prob - delta)).astype(BF16)
            o_s[b, :, cols] = untwo(mm(vals, prob_b, 0, 0))
            dq_s[b, :, cols] = untwo(mm(keys, d_sc, 0, 0) * HD**-0.5)
            gx[:, window, cols] += mm(d_sc, qq).reshape(EXT_R, WINC, 128)
            gx[:, window, vcols] += mm(prob_b, dd).reshape(EXT_R, WINC, 128)

    def back_copy(way, p):
        ss, rs = (bn_ss, bn_rs) if way == 0 else (bs_ss, bs_rs)
        return rcopy(gns_s.at[way, p], gns_r.at[way, p], ss.at[p], rs.at[p], tile(step[way], 0), h)

    def back_ew(way):
        return rcopy(gew_s.at[way], gew_r.at[way], be_ss.at[way], be_rs.at[way], tile(0, step[way]), h)

    def give(p):
        for way in range(2):
            rows = slice(0, RAD) if way == 0 else slice(RAD + TH, EXT_R)

            def send(way=way, rows=rows):
                value = gx[rows, p * BW : (p + 1) * BW, :].reshape(SLAB, 2 * WID)
                gns_s[way, p] = value.astype(BF16)
                back_copy(way, p).start()

            pl.when(can_send[way])(send)

    def fold(p):
        for way in range(2):
            rows = slice(TH, RAD + TH) if way == 0 else slice(RAD, 2 * RAD)

            def add(way=way, rows=rows):
                back_copy(way, p).wait_recv()
                value = gns_r[way, p].astype(F32).reshape(RAD, BW, 2 * WID)
                gx[rows, p * BW : (p + 1) * BW, :] += value

            pl.when(can_recv[way])(add)

    def give_ew(way):
        cols = slice(0, PAD) if way == 0 else slice(PAD + TW, EXT_C)
        gew_s[way] = gx[body, cols, :].reshape(EDGE, 2 * WID).astype(BF16)
        back_ew(way).start()

    def fold_ew(way):
        cols = slice(TW, TW + PAD) if way == 0 else slice(PAD, 2 * PAD)
        back_ew(way).wait_recv()
        gx[body, cols, :] += gew_r[way].astype(F32).reshape(TH, PAD, 2 * WID)

    for c in ORDER:
        if c != 3:
            take_chunk(c)
    block(1)
    take_corners(1)
    block(0)
    give(0)
    give(1)
    take_chunk(3)
    take_corners(0)
    block(3)
    give(4)
    block(2)
    give(2)
    give(3)

    def e_chunk(chunk):
        dq = dq_s[...].reshape(ROWS, WID)
        oo = o_s[...].reshape(ROWS, WID)
        return jnp.concatenate([mm(xt[chunk], dq), mm(gt[chunk], oo)], axis=1)

    def e_copy(k):
        return rcopy(e_s.at[k], e_r.at[k], e_ss.at[k], e_rs.at[k], tile(0, k + 1), h)

    def l_copy(k):
        return rcopy(l_s.at[k], l_r.at[k], l_ss.at[k], l_rs.at[k], tile(0, k + 1), h)

    def e_step(k, carry):
        e_s[k] = e_chunk(lax.rem(lon + k + 1, LON)).astype(BF16)
        e_copy(k).start()
        return carry

    lax.fori_loop(0, LON - 1, e_step, 0)
    own_e[...] = e_chunk(lon)
    fold(0)
    give_ew(0)
    fold(4)
    give_ew(1)

    for s in range(4):
        tacc[s] = mm(dq_s[...].reshape(ROWS, WID), w_v[0, s], 1, 1)

    for p in (1, 2, 3):
        fold(p)
    for way in range(2):
        fold_ew(way)
    for c in range(NB):
        value = gx[body, PAD + c * BW : PAD + (c + 1) * BW, :].reshape(QN, 2 * WID)
        dkv[c * QN : (c + 1) * QN, :] = value.astype(BF16)

    def l_step(k, carry):
        l_s[k] = mm(xt[lax.rem(lon + k + 1, LON)], dkv[...]).astype(BF16)
        l_copy(k).start()
        return carry

    lax.fori_loop(0, LON - 1, l_step, 0)
    own_l[...] = mm(xt[lon], dkv[...])

    def t_full(s):
        return (
            tacc[s]
            + mm(dkv[:, 0:WID], w_v[1, s], 1, 1)
            + mm(dkv[:, WID : 2 * WID], w_v[2, s], 1, 1)
        )

    t_opp = rcopy(t_s.at[0], t_r.at[0], t_ss.at[0], t_rs.at[0], g, sib)
    t_sib = rcopy(t_s.at[1], t_r.at[1], t_ss.at[1], t_rs.at[1], g, sib)
    t_far = rcopy(t_s.at[2], t_r.at[2], t_ss.at[2], t_rs.at[2], g, far)
    t_s[0] = t_full(opp).astype(BF16)
    t_opp.start()
    t_s[1] = t_full(sib).astype(BF16)
    t_sib.start()
    far_part = t_full(far)
    t_opp.wait_recv()
    t_s[2] = (far_part + t_r[0].astype(F32)).astype(BF16)
    t_far.start()
    tacc[h] = t_full(h)

    def e2_copy(k):
        to = lax.rem(lat + k + 1, LAT)
        rows = pl.ds(pl.multiple_of(to * 16, 16), 16)
        return rcopy(pe_b.at[rows], e2_r.at[k], e2_ss.at[k], e2_rs.at[k], tile(k + 1, 0), h)

    def l2_copy(k):
        to = lax.rem(lat + k + 1, LAT)
        rows = pl.ds(pl.multiple_of(to * 16, 16), 16)
        return rcopy(pl_b.at[rows], l2_r.at[k], l2_ss.at[k], l2_rs.at[k], tile(k + 1, 0), h)

    def level(own, first_copy, recv, packed, second_copy):
        def add(k, carry):
            first_copy(k).wait_recv()
            own[...] += recv[k].astype(F32)
            return carry

        lax.fori_loop(0, LON - 1, add, 0)
        packed[...] = own[...].astype(BF16)

        def send(k, carry):
            second_copy(k).start()
            return carry

        lax.fori_loop(0, LAT - 1, send, 0)

    level(own_e, e_copy, e_r, pe_b, e2_copy)
    level(own_l, l_copy, l_r, pl_b, l2_copy)

    t_sib.wait_recv()
    t_far.wait_recv()
    for c in range(NB):
        rows = slice(c * QN, (c + 1) * QN)
        total = tacc[h, rows] + t_r[1, rows].astype(F32) + t_r[2, rows].astype(F32)
        tok_ref[:, c * BW : (c + 1) * BW, :] = total.astype(BF16).reshape(TH, BW, WID)

    def finish(out, own, second_copy, recv):
        out[...] = own[pl.ds(pl.multiple_of(lat * 16, 16), 16), :]

        def add(k, carry):
            second_copy(k).wait_recv()
            out[...] += recv[k].astype(F32)
            return carry

        lax.fori_loop(0, LAT - 1, add, 0)

    finish(eo_ref, own_e, e2_copy, e2_r)
    finish(lo_ref, own_l, l2_copy, l2_r)

    for copies in x_copies + g_copies + [(t_opp, t_sib, t_far)]:
        for copy in copies:
            copy.wait_send()
    for way in range(2):
        ew_copy(way).wait_send()
        back_ew(way).wait_send()

        def sent(way=way):
            for c in range(NB):
                ns_copy(way, c).wait_send()
            for side in range(2):
                corner_copy(way, side).wait_send()
            for p in range(PIECES):
                back_copy(way, p).wait_send()

        pl.when(can_send[way])(sent)

    def drain(k, carry):
        e_copy(k).wait_send()
        l_copy(k).wait_send()
        e2_copy(k).wait_send()
        l2_copy(k).wait_send()
        return carry

    lax.fori_loop(0, LON - 1, drain, 0)


def local(tokens, qkv_weight, out_weight, out_grad):
    vm = pltpu.VMEM
    dma = pltpu.SemaphoreType.DMA
    scratch = [
        vm((3, 4, WID, WID), BF16),
        vm((WID, 4 * WID), BF16),
        vm((3, NB, TH, BW, WID), BF16),
        vm((3, NB, TH, BW, WID), BF16),
        vm((NB, QN, 2 * WID), BF16),
        vm((2, EDGE, 2 * WID), BF16),
        vm((2, NB, SLAB, 2 * WID), BF16),
        vm((2, EDGE, 2 * WID), BF16),
        vm((4, CORNER, 2 * WID), BF16),
        vm((EXT_R, EXT_C, 2 * WID), F32),
        vm((EXT_R, EXT_C, 2 * WID), F32),
        vm((NB, QN, WID), BF16),
        vm((NB, QN, WID), BF16),
        vm((NB, QN, WID), BF16),
        vm((NB, QN, WID), BF16),
        vm((ROWS, 2 * WID), BF16),
        vm((KEYS, QN), F32),
        vm((LON, 128, ROWS), BF16),
        vm((LON, 128, ROWS), BF16),
        vm((2, PIECES, SLAB, 2 * WID), BF16),
        vm((2, EDGE, 2 * WID), BF16),
        vm((2, PIECES, SLAB, 2 * WID), BF16),
        vm((2, EDGE, 2 * WID), BF16),
        vm((LON - 1, 128, 2 * WID), BF16),
        vm((LON - 1, 128, 2 * WID), BF16),
        vm((LON - 1, 128, 2 * WID), BF16),
        vm((LON - 1, 128, 2 * WID), BF16),
        vm((128, 2 * WID), F32),
        vm((128, 2 * WID), F32),
        vm((128, 2 * WID), BF16),
        vm((128, 2 * WID), BF16),
        vm((LAT - 1, 16, 2 * WID), BF16),
        vm((LAT - 1, 16, 2 * WID), BF16),
        vm((4, ROWS, WID), F32),
        vm((3, ROWS, WID), BF16),
        vm((3, ROWS, WID), BF16),
        dma((2,)),
        dma((3 * NB,)), dma((3 * NB,)),
        dma((3 * NB,)), dma((3 * NB,)),
        dma((NB,)), dma((NB,)),
        dma((NB,)), dma((NB,)),
        dma((2,)), dma((2,)),
        dma((4,)), dma((4,)),
        dma((PIECES,)), dma((PIECES,)),
        dma((PIECES,)), dma((PIECES,)),
        dma((2,)), dma((2,)),
        dma((7,)), dma((7,)),
        dma((7,)), dma((7,)),
        dma((7,)), dma((7,)),
        dma((7,)), dma((7,)),
        dma((3,)), dma((3,)),
    ]
    in_vmem = pl.BlockSpec(memory_space=pltpu.VMEM)
    anywhere = pl.BlockSpec(memory_space=pl.ANY)
    d_tok, early, late = pl.pallas_call(
        kernel,
        out_shape=(
            jax.ShapeDtypeStruct((TH, TW, WID), BF16),
            jax.ShapeDtypeStruct((16, 2 * WID), F32),
            jax.ShapeDtypeStruct((16, 2 * WID), F32),
        ),
        in_specs=[in_vmem, in_vmem, anywhere, anywhere],
        out_specs=(in_vmem, in_vmem, in_vmem),
        scratch_shapes=scratch,
        compiler_params=pltpu.CompilerParams(
            collective_id=0, has_side_effects=True, vmem_limit_bytes=56 * 1024 * 1024
        ),
        cost_estimate=pl.CostEstimate(flops=8_000_000_000, bytes_accessed=4_000_000, transcendentals=1_400_000),
    )(
        tokens.reshape(TH, TW, WID),
        out_grad.reshape(TH, TW, WID),
        qkv_weight.reshape(3, 4, WID, WID),
        out_weight,
    )
    d_qkv = jnp.stack([early[:, :WID], late[:, :WID], late[:, WID:]])
    return d_tok.reshape(tokens.shape), d_qkv, early[:, WID:].T


def solution(mesh):
    in_specs = (
        P("grid", None, None, "heads"),
        P(None, None, "heads"),
        P("heads", None),
        P("grid", None, None, "heads"),
    )
    out_specs = (P("grid", None, None, "heads"), P(None, "grid", "heads"), P("heads", "grid"))
    return jax.shard_map(local, mesh=mesh, in_specs=in_specs, out_specs=out_specs, check_vma=False)
```

```python
import jax
import jax.numpy as jnp
from jax import lax
from jax.experimental import pallas as pl
from jax.experimental.pallas import tpu as pltpu
from jax.sharding import PartitionSpec as P

MESH = pl.DeviceIdType.MESH
F32 = jnp.float32
BF16 = jnp.bfloat16

HD = 64
RAD = 6
LON = 8
LAT = 8
TH = 8
TW = 64
WID = 256
ROWS = TH * TW
EXT_R = TH + 2 * RAD
PAD = 8
EXT_C = TW + 2 * PAD
BW = 16
WINC = BW + 2 * PAD
KEYS = EXT_R * WINC
QN = TH * BW
NB = TW // BW
SLAB = RAD * BW
EDGE = TH * PAD
CORNER = RAD * PAD
PIECES = EXT_C // BW
ORDER = (0, 3, 1, 2)
BLOCKS = (1, 0, 3, 2)
DIRECT = 384


def mm(a, b, ca=1, cb=0):
    return lax.dot_general(a, b, (((ca,), (cb,)), ((), ())), preferred_element_type=F32)


def kernel(
    x_ref, g_ref, w_any, wo_any,
    tok_ref, dqkv_ref, dwo_ref,
    w_v, wo_v, xf, gf, kvb, edge, ns_r, ew_r, co_r, kvx, gx,
    q_s, do_s, o_s, dq_s, dkv, bias, xt, gt,
    gns_s, gew_s, gns_r, gew_r,
    e_s, e_r, l_s, l_r, own_e, own_l, pe_b, pl_b, e2_r, l2_r,
    m_s, m_f, m_r, own_m, pm_b, m2_r,
    tacc, t_s, t_r,
    w_sem, x_ss, x_rs, g_ss, g_rs, n_ss, n_rs, s_ss, s_rs, ew_ss, ew_rs, co_ss, co_rs,
    bn_ss, bn_rs, bs_ss, bs_rs, be_ss, be_rs,
    e_ss, e_rs, l_ss, l_rs, e2_ss, e2_rs, l2_ss, l2_rs, m_ss, m_rs, m2_ss, m2_rs, t_ss, t_rs,
):
    g = lax.axis_index("grid")
    h = lax.axis_index("heads")
    lat = lax.rem(g, LAT)
    lon = lax.div(g, LAT)
    sib = h + 1 - 2 * lax.rem(h, 2)
    far = h + 2 - 4 * lax.div(h, 2)
    opp = 3 - h
    slots = (h, sib, far, opp)

    w_copy = pltpu.make_async_copy(w_any, w_v, w_sem.at[0])
    wo_copy = pltpu.make_async_copy(wo_any, wo_v, w_sem.at[1])
    w_copy.start()
    wo_copy.start()

    def tile(dlat, dlon):
        return lax.rem(lon + dlon + LON, LON) * LAT + lax.rem(lat + dlat + LAT, LAT)

    has_n = lat > 0
    has_s = lat < LAT - 1
    can_send = (has_n, has_s)
    can_recv = (has_s, has_n)
    step = (-1, 1)

    bar = pltpu.get_barrier_semaphore()

    def greet(to_grid, to_head):
        pl.semaphore_signal(bar, inc=1, device_id=(to_grid, to_head), device_id_type=MESH)

    greet(g, sib)
    greet(g, far)
    for k in range(1, 8):
        greet(tile(k, 0), h)
        greet(tile(0, k), h)
    pl.semaphore_wait(bar, 16)

    def rcopy(src, dst, ss, rs, to_grid, to_head):
        return pltpu.make_async_remote_copy(
            src_ref=src, dst_ref=dst, send_sem=ss, recv_sem=rs,
            device_id=(to_grid, to_head), device_id_type=MESH,
        )

    def gather(src, full, ss, rs, c):
        mine = src.at[:, c * BW : (c + 1) * BW, :]
        return (
            rcopy(mine, full.at[0, c], ss.at[c], rs.at[c], g, sib),
            rcopy(mine, full.at[1, c], ss.at[NB + c], rs.at[NB + c], g, far),
            rcopy(full.at[1, c], full.at[2, c], ss.at[2 * NB + c], rs.at[2 * NB + c], g, sib),
        )

    x_copies = [gather(x_ref, xf, x_ss, x_rs, c) for c in range(NB)]
    g_copies = [gather(g_ref, gf, g_ss, g_rs, c) for c in range(NB)]
    for c in ORDER:
        x_copies[c][1].start()
        x_copies[c][0].start()

    def chunk_of(ref, full, k, c):
        value = ref[:, c * BW : (c + 1) * BW, :] if k == 0 else full[k - 1, c]
        return value.reshape(QN, WID)

    key = lax.broadcasted_iota(jnp.int32, (KEYS, QN), 0)
    qry = lax.broadcasted_iota(jnp.int32, (KEYS, QN), 1)
    key_r, key_c = lax.div(key, WINC), lax.rem(key, WINC)
    dr = key_r - lax.div(qry, BW)
    dc = key_c - lax.rem(qry, BW)
    at_lat = key_r + (lat * TH - RAD)
    fine = (dr >= 0) & (dr <= 2 * RAD) & (dc >= PAD - RAD) & (dc <= PAD + RAD)
    fine = fine & (at_lat >= 0) & (at_lat < LAT * TH)
    bias[...] = jnp.where(fine, 0.0, -1e30)

    def clear(i, carry):
        gx[i] = jnp.zeros((EXT_C, 2 * WID), F32)
        return carry

    lax.fori_loop(0, EXT_R, clear, 0)
    body = slice(RAD, RAD + TH)
    rim = (slice(RAD + TH, EXT_R), slice(0, RAD))
    for way in range(2):

        def blank(way=way):
            kvx[rim[way], :, :] = jnp.zeros((RAD, EXT_C, 2 * WID), F32)

        pl.when(jnp.logical_not(can_recv[way]))(blank)
    w_copy.wait()

    def ns_copy(way, c):
        rows = slice(0, SLAB) if way == 0 else slice(QN - SLAB, QN)
        ss, rs = (n_ss, n_rs) if way == 0 else (s_ss, s_rs)
        return rcopy(kvb.at[c, rows], ns_r.at[way, c], ss.at[c], rs.at[c], tile(step[way], 0), h)

    def ew_copy(way):
        return rcopy(edge.at[way], ew_r.at[way], ew_ss.at[way], ew_rs.at[way], tile(0, step[way]), h)

    def corner_copy(way, side):
        rows = slice(0, CORNER) if way == 0 else slice(EDGE - CORNER, EDGE)
        at = 2 * way + side
        return rcopy(ew_r.at[side, rows], co_r.at[at], co_ss.at[at], co_rs.at[at], tile(step[way], 0), h)

    def arrive(copies, c):
        copies[c][1].wait_recv()
        copies[c][2].start()

    for c in ORDER:
        total = [None, None]

        def add_kv(k, c=c, total=total):
            block = chunk_of(x_ref, xf, k, c)
            for i in range(2):
                part = mm(block, w_v[i + 1, slots[k]])
                total[i] = part if total[i] is None else total[i] + part

        add_kv(0)
        x_copies[c][0].wait_recv()
        add_kv(1)
        if c == ORDER[0]:
            arrive(x_copies, c)
        add_kv(2)
        if c != ORDER[-1]:
            arrive(x_copies, ORDER[ORDER.index(c) + 1])
        else:
            for other in BLOCKS:
                g_copies[other][1].start()
                g_copies[other][0].start()
        x_copies[c][2].wait_recv()
        add_kv(3)
        value = jnp.concatenate([total[0].astype(BF16), total[1].astype(BF16)], axis=1)
        kvb[c] = value
        for way in range(2):
            pl.when(can_send[way])(ns_copy(way, c).start)
        wide = value.astype(F32).reshape(TH, BW, 2 * WID)
        kvx[body, PAD + c * BW : PAD + (c + 1) * BW, :] = wide
        if c == 0:
            edge[0] = wide[:, :PAD, :].reshape(EDGE, 2 * WID).astype(BF16)
            ew_copy(0).start()
        if c == NB - 1:
            edge[1] = wide[:, BW - PAD :, :].reshape(EDGE, 2 * WID).astype(BF16)
            ew_copy(1).start()

    def turn(ref, full, out, c):
        for k in range(4):
            piece = chunk_of(ref, full, k, c)
            for j in range(2):
                part = piece[:, j * 128 : (j + 1) * 128].astype(F32)
                out[2 * slots[k] + j, :, c * QN : (c + 1) * QN] = part.T.astype(BF16)

    def query(c):
        total = mm(chunk_of(x_ref, xf, 0, c), w_v[0, slots[0]])
        for k in range(1, 4):
            total += mm(chunk_of(x_ref, xf, k, c), w_v[0, slots[k]])
        q_s[c] = total.astype(BF16) * jnp.asarray(HD**-0.5, BF16)

    for c in ORDER[:2]:
        query(c)
    for side in range(2):
        ew_copy(side).wait_recv()
        for way in range(2):
            pl.when(can_send[way])(corner_copy(way, side).start)
    for c in ORDER[2:]:
        query(c)
    for c in range(NB):
        turn(x_ref, xf, xt, c)
    for side in range(2):
        cols = slice(PAD + TW, EXT_C) if side == 0 else slice(0, PAD)
        kvx[body, cols, :] = ew_r[side].astype(F32).reshape(TH, PAD, 2 * WID)

    wo_copy.wait()

    def cotangent(c, after):
        g_copies[c][0].wait_recv()
        total = None
        for k in range(4):
            if k == 3:
                if after is not None:
                    arrive(g_copies, after)
                g_copies[c][2].wait_recv()
            cols = pl.ds(pl.multiple_of(slots[k] * WID, WID), WID)
            part = mm(chunk_of(g_ref, gf, k, c), wo_v[:, cols], 1, 1)
            total = part if total is None else total + part
        do_s[c] = total.astype(BF16)
        turn(g_ref, gf, gt, c)

    def take_chunk(c):
        for way in range(2):

            def take(way=way):
                ns_copy(way, c).wait_recv()
                value = ns_r[way, c].astype(F32).reshape(RAD, BW, 2 * WID)
                kvx[rim[way], PAD + c * BW : PAD + (c + 1) * BW, :] = value

            pl.when(can_recv[way])(take)

    def take_corners(side):
        cols = slice(PAD + TW, EXT_C) if side == 0 else slice(0, PAD)
        for way in range(2):

            def take(way=way):
                corner_copy(way, side).wait_recv()
                kvx[rim[way], cols, :] = co_r[2 * way + side].astype(F32).reshape(RAD, PAD, 2 * WID)

            pl.when(can_recv[way])(take)

    lane = lax.broadcasted_iota(jnp.int32, (QN, 128), 1)
    first = lane < HD

    def two_heads(value):
        zero = jnp.zeros_like(value)
        return jnp.concatenate([jnp.where(first, value, zero), jnp.where(first, zero, value)], axis=0)

    def untwo(value):
        picked = jnp.concatenate([value[:HD, :QN], value[HD:, QN:]], axis=0)
        return picked.T.astype(BF16)

    def block(b):
        window = slice(b * BW, b * BW + WINC)
        for p in range(2):
            cols = slice(p * 128, (p + 1) * 128)
            vcols = slice(WID + p * 128, WID + (p + 1) * 128)
            keys = kvx[:, window, cols].reshape(KEYS, 128).astype(BF16)
            vals = kvx[:, window, vcols].reshape(KEYS, 128).astype(BF16)
            qq = two_heads(q_s[b, :, cols])
            dd = two_heads(do_s[b, :, cols])
            scores = mm(keys, qq, 1, 1)
            b1 = bias[...]
            raw = jnp.exp(scores + jnp.concatenate([b1, b1], axis=1))
            prob = raw * (1.0 / jnp.sum(raw, axis=0, keepdims=True))
            prob_b = prob.astype(BF16)
            d_prob = mm(vals, dd, 1, 1)
            delta = jnp.sum(prob * d_prob, axis=0, keepdims=True)
            d_sc = (prob * (d_prob - delta)).astype(BF16)
            o_s[b, :, cols] = untwo(mm(vals, prob_b, 0, 0))
            dq_s[b, :, cols] = untwo(mm(keys, d_sc, 0, 0) * HD**-0.5)
            gx[:, window, cols] += mm(d_sc, qq).reshape(EXT_R, WINC, 128)
            gx[:, window, vcols] += mm(prob_b, dd).reshape(EXT_R, WINC, 128)

    def back_copy(way, p):
        ss, rs = (bn_ss, bn_rs) if way == 0 else (bs_ss, bs_rs)
        return rcopy(gns_s.at[way, p], gns_r.at[way, p], ss.at[p], rs.at[p], tile(step[way], 0), h)

    def back_ew(way):
        return rcopy(gew_s.at[way], gew_r.at[way], be_ss.at[way], be_rs.at[way], tile(0, step[way]), h)

    def give(p):
        for way in range(2):
            rows = slice(0, RAD) if way == 0 else slice(RAD + TH, EXT_R)

            def send(way=way, rows=rows):
                value = gx[rows, p * BW : (p + 1) * BW, :].reshape(SLAB, 2 * WID)
                gns_s[way, p] = value.astype(BF16)
                back_copy(way, p).start()

            pl.when(can_send[way])(send)

    def fold(p):
        for way in range(2):
            rows = slice(TH, RAD + TH) if way == 0 else slice(RAD, 2 * RAD)

            def add(way=way, rows=rows):
                back_copy(way, p).wait_recv()
                value = gns_r[way, p].astype(F32).reshape(RAD, BW, 2 * WID)
                gx[rows, p * BW : (p + 1) * BW, :] += value

            pl.when(can_recv[way])(add)

    def give_ew(way):
        cols = slice(0, PAD) if way == 0 else slice(PAD + TW, EXT_C)
        gew_s[way] = gx[body, cols, :].reshape(EDGE, 2 * WID).astype(BF16)
        back_ew(way).start()

    def fold_ew(way):
        cols = slice(TW, TW + PAD) if way == 0 else slice(PAD, 2 * PAD)
        back_ew(way).wait_recv()
        gx[body, cols, :] += gew_r[way].astype(F32).reshape(TH, PAD, 2 * WID)

    arrive(g_copies, 1)
    cotangent(1, 0)
    for c in (0, 1, 2):
        take_chunk(c)
    block(1)
    cotangent(0, 3)
    take_corners(1)
    block(0)
    give(0)
    give(1)
    cotangent(3, 2)
    take_chunk(3)
    take_corners(0)
    block(3)
    give(4)
    cotangent(2, None)
    block(2)
    give(2)
    give(3)

    def e_chunk(chunk):
        dq = dq_s[...].reshape(ROWS, WID)
        oo = o_s[...].reshape(ROWS, WID)
        return jnp.concatenate([mm(xt[chunk], dq), mm(gt[chunk], oo)], axis=1)

    def e_copy(k):
        return rcopy(e_s.at[k], e_r.at[k], e_ss.at[k], e_rs.at[k], tile(0, k + 1), h)

    def l_copy(k):
        return rcopy(l_s.at[k], l_r.at[k], l_ss.at[k], l_rs.at[k], tile(0, k + 1), h)

    def e_step(k, carry):
        e_s[k] = e_chunk(lax.rem(lon + k + 1, LON)).astype(BF16)
        e_copy(k).start()
        return carry

    lax.fori_loop(0, LON - 1, e_step, 0)
    own_e[...] = e_chunk(lon)
    fold(0)
    give_ew(0)
    fold(4)
    give_ew(1)

    for s in range(4):
        tacc[s] = mm(dq_s[...].reshape(ROWS, WID), w_v[0, s], 1, 1)

    for p in (1, 2, 3):
        fold(p)
    for way in range(2):
        fold_ew(way)
    for c in range(NB):
        value = gx[body, PAD + c * BW : PAD + (c + 1) * BW, :].reshape(QN, 2 * WID)
        dkv[c * QN : (c + 1) * QN, :] = value.astype(BF16)

    def m_copy(k):
        to = lax.rem(lat + k + 1, LAT)
        rows = pl.ds(pl.multiple_of(to * 16, 16), 16)
        return rcopy(m_s.at[:, rows], m_r.at[k], m_ss.at[k], m_rs.at[k], tile(k + 1, 0), h)

    def l_step(k, carry):
        l_s[k] = mm(xt[lax.rem(lon + k + 1, LON)], dkv[:, :DIRECT]).astype(BF16)
        l_copy(k).start()
        return carry

    def m_step(k, carry):
        full = mm(xt[k], dkv[:, DIRECT:])
        m_s[k] = full.astype(BF16)
        m_f[k] = full
        return carry

    lax.fori_loop(0, LON - 1, l_step, 0)
    lax.fori_loop(0, LON, m_step, 0)
    for k in range(LAT - 1):
        m_copy(k).start()
    own_l[...] = mm(xt[lon], dkv[:, :DIRECT])

    def t_full(s):
        return (
            tacc[s]
            + mm(dkv[:, 0:WID], w_v[1, s], 1, 1)
            + mm(dkv[:, WID : 2 * WID], w_v[2, s], 1, 1)
        )

    t_opp = rcopy(t_s.at[0], t_r.at[0], t_ss.at[0], t_rs.at[0], g, sib)
    t_sib = rcopy(t_s.at[1], t_r.at[1], t_ss.at[1], t_rs.at[1], g, sib)
    t_far = rcopy(t_s.at[2], t_r.at[2], t_ss.at[2], t_rs.at[2], g, far)
    t_s[0] = t_full(opp).astype(BF16)
    t_opp.start()
    t_s[1] = t_full(sib).astype(BF16)
    t_sib.start()
    far_part = t_full(far)
    t_opp.wait_recv()
    t_s[2] = (far_part + t_r[0].astype(F32)).astype(BF16)
    t_far.start()
    tacc[h] = t_full(h)

    def e2_copy(k):
        to = lax.rem(lat + k + 1, LAT)
        rows = pl.ds(pl.multiple_of(to * 16, 16), 16)
        return rcopy(pe_b.at[rows], e2_r.at[k], e2_ss.at[k], e2_rs.at[k], tile(k + 1, 0), h)

    def l2_copy(k):
        to = lax.rem(lat + k + 1, LAT)
        rows = pl.ds(pl.multiple_of(to * 16, 16), 16)
        return rcopy(pl_b.at[rows], l2_r.at[k], l2_ss.at[k], l2_rs.at[k], tile(k + 1, 0), h)

    def level(own, first_copy, recv, packed, second_copy):
        def add(k, carry):
            first_copy(k).wait_recv()
            own[...] += recv[k].astype(F32)
            return carry

        lax.fori_loop(0, LON - 1, add, 0)
        packed[...] = own[...].astype(BF16)

        def send(k, carry):
            second_copy(k).start()
            return carry

        lax.fori_loop(0, LAT - 1, send, 0)

    def m2_copy(k):
        to = lax.rem(lon + k + 1, LON)
        return rcopy(pm_b.at[to], m2_r.at[k], m2_ss.at[k], m2_rs.at[k], tile(0, k + 1), h)

    level(own_e, e_copy, e_r, pe_b, e2_copy)

    here = pl.ds(pl.multiple_of(lat * 16, 16), 16)
    total = m_f[:, here, :]
    for k in range(LAT - 1):
        m_copy(k).wait_recv()
        total += m_r[k].astype(F32)
    pm_b[...] = total.astype(BF16)
    own_m[...] = total
    for k in range(LON - 1):
        m2_copy(k).start()

    level(own_l, l_copy, l_r, pl_b, l2_copy)

    t_sib.wait_recv()
    t_far.wait_recv()
    for c in range(NB):
        rows = slice(c * QN, (c + 1) * QN)
        total = tacc[h, rows] + t_r[1, rows].astype(F32) + t_r[2, rows].astype(F32)
        tok_ref[:, c * BW : (c + 1) * BW, :] = total.astype(BF16).reshape(TH, BW, WID)

    def finish(own, second_copy, recv):
        total = own[here, :]
        for k in range(LAT - 1):
            second_copy(k).wait_recv()
            total += recv[k].astype(F32)
        return total

    early = finish(own_e, e2_copy, e2_r)
    dqkv_ref[0] = early[:, :WID]
    dwo_ref[...] = early[:, WID:]
    last = own_m[lon]
    for k in range(LON - 1):
        m2_copy(k).wait_recv()
        last += m2_r[k].astype(F32)
    dqkv_ref[2, :, WID - 128 :] = last
    late = finish(own_l, l2_copy, l2_r)
    dqkv_ref[1] = late[:, :WID]
    dqkv_ref[2, :, : WID - 128] = late[:, WID:]

    for copies in x_copies + g_copies + [(t_opp, t_sib, t_far)]:
        for copy in copies:
            copy.wait_send()
    for way in range(2):
        ew_copy(way).wait_send()
        back_ew(way).wait_send()

        def sent(way=way):
            for c in range(NB):
                ns_copy(way, c).wait_send()
            for side in range(2):
                corner_copy(way, side).wait_send()
            for p in range(PIECES):
                back_copy(way, p).wait_send()

        pl.when(can_send[way])(sent)

    def drain(k, carry):
        e_copy(k).wait_send()
        l_copy(k).wait_send()
        e2_copy(k).wait_send()
        l2_copy(k).wait_send()
        m_copy(k).wait_send()
        m2_copy(k).wait_send()
        return carry

    lax.fori_loop(0, LON - 1, drain, 0)


def hand_out(tok_in, dqkv_in, dwo_in, tok_ref, dqkv_ref, dwo_ref):
    tok_ref[...] = tok_in[...]
    dqkv_ref[...] = dqkv_in[...]
    dwo_ref[...] = dwo_in[...]


def local(tokens, qkv_weight, out_weight, out_grad):
    vm = pltpu.VMEM
    dma = pltpu.SemaphoreType.DMA
    scratch = [
        vm((3, 4, WID, WID), BF16),
        vm((WID, 4 * WID), BF16),
        vm((3, NB, TH, BW, WID), BF16),
        vm((3, NB, TH, BW, WID), BF16),
        vm((NB, QN, 2 * WID), BF16),
        vm((2, EDGE, 2 * WID), BF16),
        vm((2, NB, SLAB, 2 * WID), BF16),
        vm((2, EDGE, 2 * WID), BF16),
        vm((4, CORNER, 2 * WID), BF16),
        vm((EXT_R, EXT_C, 2 * WID), F32),
        vm((EXT_R, EXT_C, 2 * WID), F32),
        vm((NB, QN, WID), BF16),
        vm((NB, QN, WID), BF16),
        vm((NB, QN, WID), BF16),
        vm((NB, QN, WID), BF16),
        vm((ROWS, 2 * WID), BF16),
        vm((KEYS, QN), F32),
        vm((LON, 128, ROWS), BF16),
        vm((LON, 128, ROWS), BF16),
        vm((2, PIECES, SLAB, 2 * WID), BF16),
        vm((2, EDGE, 2 * WID), BF16),
        vm((2, PIECES, SLAB, 2 * WID), BF16),
        vm((2, EDGE, 2 * WID), BF16),
        vm((LON - 1, 128, 2 * WID), BF16),
        vm((LON - 1, 128, 2 * WID), BF16),
        vm((LON - 1, 128, DIRECT), BF16),
        vm((LON - 1, 128, DIRECT), BF16),
        vm((128, 2 * WID), F32),
        vm((128, DIRECT), F32),
        vm((128, 2 * WID), BF16),
        vm((128, DIRECT), BF16),
        vm((LAT - 1, 16, 2 * WID), BF16),
        vm((LAT - 1, 16, DIRECT), BF16),
        vm((LON, 128, 128), BF16),
        vm((LON, 128, 128), F32),
        vm((LAT - 1, LON, 16, 128), BF16),
        vm((LON, 16, 128), F32),
        vm((LON, 16, 128), BF16),
        vm((LON - 1, 16, 128), BF16),
        vm((4, ROWS, WID), F32),
        vm((3, ROWS, WID), BF16),
        vm((3, ROWS, WID), BF16),
        dma((2,)),
        dma((3 * NB,)), dma((3 * NB,)),
        dma((3 * NB,)), dma((3 * NB,)),
        dma((NB,)), dma((NB,)),
        dma((NB,)), dma((NB,)),
        dma((2,)), dma((2,)),
        dma((4,)), dma((4,)),
        dma((PIECES,)), dma((PIECES,)),
        dma((PIECES,)), dma((PIECES,)),
        dma((2,)), dma((2,)),
        dma((7,)), dma((7,)),
        dma((7,)), dma((7,)),
        dma((7,)), dma((7,)),
        dma((7,)), dma((7,)),
        dma((7,)), dma((7,)),
        dma((7,)), dma((7,)),
        dma((3,)), dma((3,)),
    ]
    in_vmem = pl.BlockSpec(memory_space=pltpu.VMEM)
    anywhere = pl.BlockSpec(memory_space=pl.ANY)
    d_tok, d_qkv, d_wo = pl.pallas_call(
        kernel,
        out_shape=(
            jax.ShapeDtypeStruct((TH, TW, WID), BF16),
            jax.ShapeDtypeStruct((3, 16, WID), F32),
            jax.ShapeDtypeStruct((16, WID), F32),
        ),
        in_specs=[in_vmem, in_vmem, anywhere, anywhere],
        out_specs=(in_vmem, in_vmem, in_vmem),
        scratch_shapes=scratch,
        compiler_params=pltpu.CompilerParams(
            collective_id=0, has_side_effects=True, vmem_limit_bytes=56 * 1024 * 1024
        ),
        cost_estimate=pl.CostEstimate(flops=8_000_000_000, bytes_accessed=4_000_000, transcendentals=1_400_000),
    )(
        tokens.reshape(TH, TW, WID),
        out_grad.reshape(TH, TW, WID),
        qkv_weight.reshape(3, 4, WID, WID),
        out_weight,
    )
    d_tok, d_qkv, d_wo = pl.pallas_call(
        hand_out,
        out_shape=(
            jax.ShapeDtypeStruct((TH, TW, WID), BF16),
            jax.ShapeDtypeStruct((3, 16, WID), F32),
            jax.ShapeDtypeStruct((16, WID), F32),
        ),
        in_specs=[in_vmem] * 3,
        out_specs=(in_vmem, in_vmem, in_vmem),
    )(d_tok, d_qkv, d_wo)
    return d_tok.reshape(tokens.shape), d_qkv, d_wo.T


def solution(mesh):
    in_specs = (
        P("grid", None, None, "heads"),
        P(None, None, "heads"),
        P("heads", None),
        P("grid", None, None, "heads"),
    )
    out_specs = (P("grid", None, None, "heads"), P(None, "grid", "heads"), P("heads", "grid"))
    return jax.shard_map(local, mesh=mesh, in_specs=in_specs, out_specs=out_specs, check_vma=False)
```

```python
import jax
import jax.numpy as jnp
from jax import lax
from jax.experimental import pallas as pl
from jax.experimental.pallas import tpu as pltpu
from jax.sharding import PartitionSpec as P

MESH = pl.DeviceIdType.MESH
F32 = jnp.float32
BF16 = jnp.bfloat16

HD = 64
RAD = 6
LON = 8
LAT = 8
TH = 8
TW = 64
WID = 256
ROWS = TH * TW
EXT_R = TH + 2 * RAD
PAD = 8
EXT_C = TW + 2 * PAD
BW = 16
WINC = BW + 2 * PAD
KEYS = EXT_R * WINC
QN = TH * BW
NB = TW // BW
SLAB = RAD * BW
EDGE = TH * PAD
CORNER = RAD * PAD
PIECES = EXT_C // BW
ORDER = (0, 3, 1, 2)
BLOCKS = (1, 0, 3, 2)
DIRECT = 384


def mm(a, b, ca=1, cb=0):
    return lax.dot_general(a, b, (((ca,), (cb,)), ((), ())), preferred_element_type=F32)


def kernel(
    x_any, g_any, w_any, wo_any,
    tok_ref, dqkv_ref, dwo_ref,
    x_ref, g_ref, w_v, wo_v, xf, gf, kvb, edge, ns_r, ew_r, co_r, kvx, gx,
    q_s, do_s, o_s, dq_s, dkv, bias, xt, gt,
    gns_s, gew_s, gns_r, gew_r,
    e_s, e_r, l_s, l_r, own_e, own_l, pe_b, pl_b, e2_r, l2_r,
    m_s, m_f, m_r, own_m, pm_b, m2_r, own_3, e3_s, e3_r,
    tacc, t_s, t_r,
    w_sem, x_ss, x_rs, g_ss, g_rs, n_ss, n_rs, s_ss, s_rs, ew_ss, ew_rs, co_ss, co_rs,
    bn_ss, bn_rs, bs_ss, bs_rs, be_ss, be_rs,
    e_ss, e_rs, l_ss, l_rs, e2_ss, e2_rs, l2_ss, l2_rs, m_ss, m_rs, m2_ss, m2_rs, t_ss, t_rs, e3_sem,
):
    g = lax.axis_index("grid")
    h = lax.axis_index("heads")
    lat = lax.rem(g, LAT)
    lon = lax.div(g, LAT)
    sib = h + 1 - 2 * lax.rem(h, 2)
    far = h + 2 - 4 * lax.div(h, 2)
    opp = 3 - h
    slots = (h, sib, far, opp)

    x_load = pltpu.make_async_copy(x_any, x_ref, w_sem.at[2])
    g_load = pltpu.make_async_copy(g_any, g_ref, w_sem.at[3])
    w_copy = pltpu.make_async_copy(w_any, w_v, w_sem.at[0])
    wo_copy = pltpu.make_async_copy(wo_any, wo_v, w_sem.at[1])
    x_load.start()
    w_copy.start()
    g_load.start()
    wo_copy.start()

    def tile(dlat, dlon):
        return lax.rem(lon + dlon + LON, LON) * LAT + lax.rem(lat + dlat + LAT, LAT)

    has_n = lat > 0
    has_s = lat < LAT - 1
    can_send = (has_n, has_s)
    can_recv = (has_s, has_n)
    step = (-1, 1)

    bar = pltpu.get_barrier_semaphore()

    def greet(to_grid, to_head):
        pl.semaphore_signal(bar, inc=1, device_id=(to_grid, to_head), device_id_type=MESH)

    greet(g, sib)
    greet(g, far)
    for k in range(1, 8):
        greet(tile(k, 0), h)
        greet(tile(0, k), h)
    x_load.wait()
    pl.semaphore_wait(bar, 16)

    def rcopy(src, dst, ss, rs, to_grid, to_head):
        return pltpu.make_async_remote_copy(
            src_ref=src, dst_ref=dst, send_sem=ss, recv_sem=rs,
            device_id=(to_grid, to_head), device_id_type=MESH,
        )

    def gather(src, full, ss, rs, c):
        mine = src.at[:, c * BW : (c + 1) * BW, :]
        return (
            rcopy(mine, full.at[0, c], ss.at[c], rs.at[c], g, sib),
            rcopy(mine, full.at[1, c], ss.at[NB + c], rs.at[NB + c], g, far),
            rcopy(full.at[1, c], full.at[2, c], ss.at[2 * NB + c], rs.at[2 * NB + c], g, sib),
        )

    x_copies = [gather(x_ref, xf, x_ss, x_rs, c) for c in range(NB)]
    g_copies = [gather(g_ref, gf, g_ss, g_rs, c) for c in range(NB)]
    for c in ORDER:
        x_copies[c][1].start()
        x_copies[c][0].start()

    def chunk_of(ref, full, k, c):
        value = ref[:, c * BW : (c + 1) * BW, :] if k == 0 else full[k - 1, c]
        return value.reshape(QN, WID)

    key = lax.broadcasted_iota(jnp.int32, (KEYS, QN), 0)
    qry = lax.broadcasted_iota(jnp.int32, (KEYS, QN), 1)
    key_r, key_c = lax.div(key, WINC), lax.rem(key, WINC)
    dr = key_r - lax.div(qry, BW)
    dc = key_c - lax.rem(qry, BW)
    at_lat = key_r + (lat * TH - RAD)
    fine = (dr >= 0) & (dr <= 2 * RAD) & (dc >= PAD - RAD) & (dc <= PAD + RAD)
    fine = fine & (at_lat >= 0) & (at_lat < LAT * TH)
    bias[...] = jnp.where(fine, 0.0, -1e30)

    def clear(i, carry):
        gx[i] = jnp.zeros((EXT_C, 2 * WID), F32)
        return carry

    lax.fori_loop(0, EXT_R, clear, 0)
    body = slice(RAD, RAD + TH)
    rim = (slice(RAD + TH, EXT_R), slice(0, RAD))
    for way in range(2):

        def blank(way=way):
            kvx[rim[way], :, :] = jnp.zeros((RAD, EXT_C, 2 * WID), F32)

        pl.when(jnp.logical_not(can_recv[way]))(blank)
    w_copy.wait()
    g_load.wait()

    def ns_copy(way, c):
        rows = slice(0, SLAB) if way == 0 else slice(QN - SLAB, QN)
        ss, rs = (n_ss, n_rs) if way == 0 else (s_ss, s_rs)
        return rcopy(kvb.at[c, rows], ns_r.at[way, c], ss.at[c], rs.at[c], tile(step[way], 0), h)

    def ew_copy(way):
        return rcopy(edge.at[way], ew_r.at[way], ew_ss.at[way], ew_rs.at[way], tile(0, step[way]), h)

    def corner_copy(way, side):
        rows = slice(0, CORNER) if way == 0 else slice(EDGE - CORNER, EDGE)
        at = 2 * way + side
        return rcopy(ew_r.at[side, rows], co_r.at[at], co_ss.at[at], co_rs.at[at], tile(step[way], 0), h)

    def arrive(copies, c):
        copies[c][1].wait_recv()
        copies[c][2].start()

    for c in ORDER:
        total = [None, None]

        def add_kv(k, c=c, total=total):
            block = chunk_of(x_ref, xf, k, c)
            for i in range(2):
                part = mm(block, w_v[i + 1, slots[k]])
                total[i] = part if total[i] is None else total[i] + part

        add_kv(0)
        x_copies[c][0].wait_recv()
        add_kv(1)
        if c == ORDER[0]:
            arrive(x_copies, c)
        add_kv(2)
        if c != ORDER[-1]:
            arrive(x_copies, ORDER[ORDER.index(c) + 1])
        else:
            for other in BLOCKS:
                g_copies[other][1].start()
                g_copies[other][0].start()
        x_copies[c][2].wait_recv()
        add_kv(3)
        value = jnp.concatenate([total[0].astype(BF16), total[1].astype(BF16)], axis=1)
        kvb[c] = value
        for way in range(2):
            pl.when(can_send[way])(ns_copy(way, c).start)
        wide = value.astype(F32).reshape(TH, BW, 2 * WID)
        kvx[body, PAD + c * BW : PAD + (c + 1) * BW, :] = wide
        if c == 0:
            edge[0] = wide[:, :PAD, :].reshape(EDGE, 2 * WID).astype(BF16)
            ew_copy(0).start()
        if c == NB - 1:
            edge[1] = wide[:, BW - PAD :, :].reshape(EDGE, 2 * WID).astype(BF16)
            ew_copy(1).start()

    def turn(ref, full, out, c):
        for k in range(4):
            piece = chunk_of(ref, full, k, c)
            for j in range(2):
                part = piece[:, j * 128 : (j + 1) * 128].astype(F32)
                out[2 * slots[k] + j, :, c * QN : (c + 1) * QN] = part.T.astype(BF16)

    def query(c):
        total = mm(chunk_of(x_ref, xf, 0, c), w_v[0, slots[0]])
        for k in range(1, 4):
            total += mm(chunk_of(x_ref, xf, k, c), w_v[0, slots[k]])
        q_s[c] = total.astype(BF16) * jnp.asarray(HD**-0.5, BF16)

    for c in ORDER[:2]:
        query(c)
    for side in range(2):
        ew_copy(side).wait_recv()
        for way in range(2):
            pl.when(can_send[way])(corner_copy(way, side).start)
    for c in ORDER[2:]:
        query(c)
    for c in range(NB):
        turn(x_ref, xf, xt, c)
    for side in range(2):
        cols = slice(PAD + TW, EXT_C) if side == 0 else slice(0, PAD)
        kvx[body, cols, :] = ew_r[side].astype(F32).reshape(TH, PAD, 2 * WID)

    wo_copy.wait()

    def cotangent(c, after):
        g_copies[c][0].wait_recv()
        total = None
        for k in range(4):
            if k == 3:
                if after is not None:
                    arrive(g_copies, after)
                g_copies[c][2].wait_recv()
            cols = pl.ds(pl.multiple_of(slots[k] * WID, WID), WID)
            part = mm(chunk_of(g_ref, gf, k, c), wo_v[:, cols], 1, 1)
            total = part if total is None else total + part
        do_s[c] = total.astype(BF16)
        turn(g_ref, gf, gt, c)

    def take_chunk(c):
        for way in range(2):

            def take(way=way):
                ns_copy(way, c).wait_recv()
                value = ns_r[way, c].astype(F32).reshape(RAD, BW, 2 * WID)
                kvx[rim[way], PAD + c * BW : PAD + (c + 1) * BW, :] = value

            pl.when(can_recv[way])(take)

    def take_corners(side):
        cols = slice(PAD + TW, EXT_C) if side == 0 else slice(0, PAD)
        for way in range(2):

            def take(way=way):
                corner_copy(way, side).wait_recv()
                kvx[rim[way], cols, :] = co_r[2 * way + side].astype(F32).reshape(RAD, PAD, 2 * WID)

            pl.when(can_recv[way])(take)

    lane = lax.broadcasted_iota(jnp.int32, (QN, 128), 1)
    first = lane < HD

    def two_heads(value):
        zero = jnp.zeros_like(value)
        return jnp.concatenate([jnp.where(first, value, zero), jnp.where(first, zero, value)], axis=0)

    def untwo(value):
        picked = jnp.concatenate([value[:HD, :QN], value[HD:, QN:]], axis=0)
        return picked.T.astype(BF16)

    def block(b):
        window = slice(b * BW, b * BW + WINC)
        for p in range(2):
            cols = slice(p * 128, (p + 1) * 128)
            vcols = slice(WID + p * 128, WID + (p + 1) * 128)
            keys = kvx[:, window, cols].reshape(KEYS, 128).astype(BF16)
            vals = kvx[:, window, vcols].reshape(KEYS, 128).astype(BF16)
            qq = two_heads(q_s[b, :, cols])
            dd = two_heads(do_s[b, :, cols])
            scores = mm(keys, qq, 1, 1)
            b1 = bias[...]
            raw = jnp.exp(scores + jnp.concatenate([b1, b1], axis=1))
            prob = raw * (1.0 / jnp.sum(raw, axis=0, keepdims=True))
            prob_b = prob.astype(BF16)
            d_prob = mm(vals, dd, 1, 1)
            delta = jnp.sum(prob * d_prob, axis=0, keepdims=True)
            d_sc = (prob * (d_prob - delta)).astype(BF16)
            o_s[b, :, cols] = untwo(mm(vals, prob_b, 0, 0))
            dq_s[b, :, cols] = untwo(mm(keys, d_sc, 0, 0) * HD**-0.5)
            gx[:, window, cols] += mm(d_sc, qq).reshape(EXT_R, WINC, 128)
            gx[:, window, vcols] += mm(prob_b, dd).reshape(EXT_R, WINC, 128)

    def back_copy(way, p):
        ss, rs = (bn_ss, bn_rs) if way == 0 else (bs_ss, bs_rs)
        return rcopy(gns_s.at[way, p], gns_r.at[way, p], ss.at[p], rs.at[p], tile(step[way], 0), h)

    def back_ew(way):
        return rcopy(gew_s.at[way], gew_r.at[way], be_ss.at[way], be_rs.at[way], tile(0, step[way]), h)

    def give(p):
        for way in range(2):
            rows = slice(0, RAD) if way == 0 else slice(RAD + TH, EXT_R)

            def send(way=way, rows=rows):
                value = gx[rows, p * BW : (p + 1) * BW, :].reshape(SLAB, 2 * WID)
                gns_s[way, p] = value.astype(BF16)
                back_copy(way, p).start()

            pl.when(can_send[way])(send)

    def fold(p):
        for way in range(2):
            rows = slice(TH, RAD + TH) if way == 0 else slice(RAD, 2 * RAD)

            def add(way=way, rows=rows):
                back_copy(way, p).wait_recv()
                value = gns_r[way, p].astype(F32).reshape(RAD, BW, 2 * WID)
                gx[rows, p * BW : (p + 1) * BW, :] += value

            pl.when(can_recv[way])(add)

    def give_ew(way):
        cols = slice(0, PAD) if way == 0 else slice(PAD + TW, EXT_C)
        gew_s[way] = gx[body, cols, :].reshape(EDGE, 2 * WID).astype(BF16)
        back_ew(way).start()

    def fold_ew(way):
        cols = slice(TW, TW + PAD) if way == 0 else slice(PAD, 2 * PAD)
        back_ew(way).wait_recv()
        gx[body, cols, :] += gew_r[way].astype(F32).reshape(TH, PAD, 2 * WID)

    arrive(g_copies, 1)
    cotangent(1, 0)
    for c in (0, 1, 2):
        take_chunk(c)
    block(1)
    cotangent(0, 3)
    take_corners(1)
    block(0)
    give(0)
    give(1)
    cotangent(3, 2)
    take_chunk(3)
    take_corners(0)
    block(3)
    give(4)
    cotangent(2, None)
    block(2)
    give(2)
    give(3)

    y_at = lax.div(lon, 2)
    x_at = lax.rem(lon, 2)

    def e_part(chunk):
        dq = dq_s[...].reshape(ROWS, WID)
        oo = o_s[...].reshape(ROWS, WID)
        return jnp.concatenate([mm(xt[chunk], dq), mm(gt[chunk], oo)], axis=1)

    e_plan = ((1, 0, 1), (1, 1, -1), (0, 1, 1), (2, 0, -1), (0, 0, 1), (2, 1, -1))

    def e_copy(k):
        at, half, to = e_plan[k]
        return rcopy(e_s.at[at, half], e_r.at[k], e_ss.at[k], e_rs.at[k], tile(0, 2 * to), h)

    def l_copy(k):
        return rcopy(l_s.at[k], l_r.at[k], l_ss.at[k], l_rs.at[k], tile(0, k + 1), h)

    def e_fill(at, half):
        to = lax.rem(y_at + at + 1, LON // 2)
        e_s[at, half] = e_part(2 * to + half).astype(BF16)

    for k in range(4):
        at, half, _ = e_plan[k]
        e_fill(at, half)
        e_copy(k).start()
    e_fill(0, 0)
    e_fill(2, 1)
    for x in range(2):
        own_e[x] = e_part(2 * y_at + x)
    fold(0)
    give_ew(0)
    fold(4)
    give_ew(1)
    for k in range(2):
        e_copy(k).wait_recv()
        at, half, _ = e_plan[4 + k]
        e_s[at, half] = (e_s[at, half].astype(F32) + e_r[k].astype(F32)).astype(BF16)
        e_copy(4 + k).start()

    for s in range(4):
        tacc[s] = mm(dq_s[...].reshape(ROWS, WID), w_v[0, s], 1, 1)

    for p in (1, 2, 3):
        fold(p)
    for way in range(2):
        fold_ew(way)
    for c in range(NB):
        value = gx[body, PAD + c * BW : PAD + (c + 1) * BW, :].reshape(QN, 2 * WID)
        dkv[c * QN : (c + 1) * QN, :] = value.astype(BF16)

    def t_full(s):
        return (
            tacc[s]
            + mm(dkv[:, 0:WID], w_v[1, s], 1, 1)
            + mm(dkv[:, WID : 2 * WID], w_v[2, s], 1, 1)
        )

    t_opp = rcopy(t_s.at[0], t_r.at[0], t_ss.at[0], t_rs.at[0], g, sib)
    t_sib = rcopy(t_s.at[1], t_r.at[1], t_ss.at[1], t_rs.at[1], g, sib)
    t_far = rcopy(t_s.at[2], t_r.at[2], t_ss.at[2], t_rs.at[2], g, far)
    t_s[0] = t_full(opp).astype(BF16)
    t_opp.start()

    def m_copy(k):
        to = lax.rem(lat + k + 1, LAT)
        rows = pl.ds(pl.multiple_of(to * 16, 16), 16)
        return rcopy(m_s.at[:, rows], m_r.at[k], m_ss.at[k], m_rs.at[k], tile(k + 1, 0), h)

    def l_step(k, carry):
        l_s[k] = mm(xt[lax.rem(lon + k + 1, LON)], dkv[:, :DIRECT]).astype(BF16)
        l_copy(k).start()
        return carry

    def m_step(k, carry):
        full = mm(xt[k], dkv[:, DIRECT:])
        m_s[k] = full.astype(BF16)
        m_f[k] = full
        return carry

    lax.fori_loop(0, LON - 1, l_step, 0)
    lax.fori_loop(0, LON, m_step, 0)
    for k in range(LAT - 1):
        m_copy(k).start()
    own_l[...] = mm(xt[lon], dkv[:, :DIRECT])

    t_s[1] = t_full(sib).astype(BF16)
    t_sib.start()
    far_part = t_full(far)
    t_opp.wait_recv()
    t_s[2] = (far_part + t_r[0].astype(F32)).astype(BF16)
    t_far.start()
    tacc[h] = t_full(h)

    def e2_copy(k):
        to = lax.rem(lat + k + 1, LAT)
        rows = pl.ds(pl.multiple_of(to * 16, 16), 16)
        return rcopy(pe_b.at[:, rows], e2_r.at[k], e2_ss.at[k], e2_rs.at[k], tile(k + 1, 0), h)

    def l2_copy(k):
        to = lax.rem(lat + k + 1, LAT)
        rows = pl.ds(pl.multiple_of(to * 16, 16), 16)
        return rcopy(pl_b.at[rows], l2_r.at[k], l2_ss.at[k], l2_rs.at[k], tile(k + 1, 0), h)

    def level(own, first_copy, recv, packed, second_copy):
        def add(k, carry):
            first_copy(k).wait_recv()
            own[...] += recv[k].astype(F32)
            return carry

        lax.fori_loop(0, LON - 1, add, 0)
        packed[...] = own[...].astype(BF16)

        def send(k, carry):
            second_copy(k).start()
            return carry

        lax.fori_loop(0, LAT - 1, send, 0)

    def m2_copy(k):
        to = lax.rem(lon + k + 1, LON)
        return rcopy(pm_b.at[to], m2_r.at[k], m2_ss.at[k], m2_rs.at[k], tile(0, k + 1), h)

    for k in range(2, 6):
        e_copy(k).wait_recv()
        own_e[e_plan[k][1]] += e_r[k].astype(F32)
    pe_b[...] = own_e[...].astype(BF16)
    for k in range(LAT - 1):
        e2_copy(k).start()

    here = pl.ds(pl.multiple_of(lat * 16, 16), 16)
    total = m_f[:, here, :]
    for k in range(LAT - 1):
        m_copy(k).wait_recv()
        total += m_r[k].astype(F32)
    pm_b[...] = total.astype(BF16)
    own_m[...] = total
    for k in range(LON - 1):
        m2_copy(k).start()

    level(own_l, l_copy, l_r, pl_b, l2_copy)

    t_sib.wait_recv()
    t_far.wait_recv()
    for c in range(NB):
        rows = slice(c * QN, (c + 1) * QN)
        total = tacc[h, rows] + t_r[1, rows].astype(F32) + t_r[2, rows].astype(F32)
        tok_ref[:, c * BW : (c + 1) * BW, :] = total.astype(BF16).reshape(TH, BW, WID)

    def finish(own, second_copy, recv):
        total = own[here, :]
        for k in range(LAT - 1):
            second_copy(k).wait_recv()
            total += recv[k].astype(F32)
        return total

    early = own_e[:, here, :]
    for k in range(LAT - 1):
        e2_copy(k).wait_recv()
        early += e2_r[k].astype(F32)
    own_3[...] = early
    e3_s[...] = own_3[1 - x_at].astype(BF16)
    e3_copy = rcopy(e3_s, e3_r, e3_sem.at[0], e3_sem.at[1], tile(0, 1 - 2 * x_at), h)
    e3_copy.start()
    last = own_m[lon]
    for k in range(LON - 1):
        m2_copy(k).wait_recv()
        last += m2_r[k].astype(F32)
    dqkv_ref[2, :, WID - 128 :] = last
    late = finish(own_l, l2_copy, l2_r)
    dqkv_ref[1] = late[:, :WID]
    dqkv_ref[2, :, : WID - 128] = late[:, WID:]
    e3_copy.wait_recv()
    early = own_3[x_at] + e3_r[...].astype(F32)
    dqkv_ref[0] = early[:, :WID]
    dwo_ref[...] = early[:, WID:]

    for copies in x_copies + g_copies + [(t_opp, t_sib, t_far, e3_copy)]:
        for copy in copies:
            copy.wait_send()
    for way in range(2):
        ew_copy(way).wait_send()
        back_ew(way).wait_send()

        def sent(way=way):
            for c in range(NB):
                ns_copy(way, c).wait_send()
            for side in range(2):
                corner_copy(way, side).wait_send()
            for p in range(PIECES):
                back_copy(way, p).wait_send()

        pl.when(can_send[way])(sent)

    for k in range(6):
        e_copy(k).wait_send()

    def drain(k, carry):
        l_copy(k).wait_send()
        e2_copy(k).wait_send()
        l2_copy(k).wait_send()
        m_copy(k).wait_send()
        m2_copy(k).wait_send()
        return carry

    lax.fori_loop(0, LON - 1, drain, 0)


def hand_out(tok_in, dqkv_in, dwo_in, tok_ref, dqkv_ref, dwo_ref):
    tok_ref[...] = tok_in[...]
    dqkv_ref[...] = dqkv_in[...]
    dwo_ref[...] = dwo_in[...]


def local(tokens, qkv_weight, out_weight, out_grad):
    vm = pltpu.VMEM
    dma = pltpu.SemaphoreType.DMA
    scratch = [
        vm((TH, TW, WID), BF16),
        vm((TH, TW, WID), BF16),
        vm((3, 4, WID, WID), BF16),
        vm((WID, 4 * WID), BF16),
        vm((3, NB, TH, BW, WID), BF16),
        vm((3, NB, TH, BW, WID), BF16),
        vm((NB, QN, 2 * WID), BF16),
        vm((2, EDGE, 2 * WID), BF16),
        vm((2, NB, SLAB, 2 * WID), BF16),
        vm((2, EDGE, 2 * WID), BF16),
        vm((4, CORNER, 2 * WID), BF16),
        vm((EXT_R, EXT_C, 2 * WID), F32),
        vm((EXT_R, EXT_C, 2 * WID), F32),
        vm((NB, QN, WID), BF16),
        vm((NB, QN, WID), BF16),
        vm((NB, QN, WID), BF16),
        vm((NB, QN, WID), BF16),
        vm((ROWS, 2 * WID), BF16),
        vm((KEYS, QN), F32),
        vm((LON, 128, ROWS), BF16),
        vm((LON, 128, ROWS), BF16),
        vm((2, PIECES, SLAB, 2 * WID), BF16),
        vm((2, EDGE, 2 * WID), BF16),
        vm((2, PIECES, SLAB, 2 * WID), BF16),
        vm((2, EDGE, 2 * WID), BF16),
        vm((LON // 2 - 1, 2, 128, 2 * WID), BF16),
        vm((6, 128, 2 * WID), BF16),
        vm((LON - 1, 128, DIRECT), BF16),
        vm((LON - 1, 128, DIRECT), BF16),
        vm((2, 128, 2 * WID), F32),
        vm((128, DIRECT), F32),
        vm((2, 128, 2 * WID), BF16),
        vm((128, DIRECT), BF16),
        vm((LAT - 1, 2, 16, 2 * WID), BF16),
        vm((LAT - 1, 16, DIRECT), BF16),
        vm((LON, 128, 128), BF16),
        vm((LON, 128, 128), F32),
        vm((LAT - 1, LON, 16, 128), BF16),
        vm((LON, 16, 128), F32),
        vm((LON, 16, 128), BF16),
        vm((LON - 1, 16, 128), BF16),
        vm((2, 16, 2 * WID), F32),
        vm((16, 2 * WID), BF16),
        vm((16, 2 * WID), BF16),
        vm((4, ROWS, WID), F32),
        vm((3, ROWS, WID), BF16),
        vm((3, ROWS, WID), BF16),
        dma((4,)),
        dma((3 * NB,)), dma((3 * NB,)),
        dma((3 * NB,)), dma((3 * NB,)),
        dma((NB,)), dma((NB,)),
        dma((NB,)), dma((NB,)),
        dma((2,)), dma((2,)),
        dma((4,)), dma((4,)),
        dma((PIECES,)), dma((PIECES,)),
        dma((PIECES,)), dma((PIECES,)),
        dma((2,)), dma((2,)),
        dma((7,)), dma((7,)),
        dma((7,)), dma((7,)),
        dma((7,)), dma((7,)),
        dma((7,)), dma((7,)),
        dma((7,)), dma((7,)),
        dma((7,)), dma((7,)),
        dma((3,)), dma((3,)),
        dma((2,)),
    ]
    in_vmem = pl.BlockSpec(memory_space=pltpu.VMEM)
    anywhere = pl.BlockSpec(memory_space=pl.ANY)
    d_tok, d_qkv, d_wo = pl.pallas_call(
        kernel,
        out_shape=(
            jax.ShapeDtypeStruct((TH, TW, WID), BF16),
            jax.ShapeDtypeStruct((3, 16, WID), F32),
            jax.ShapeDtypeStruct((16, WID), F32),
        ),
        in_specs=[anywhere] * 4,
        out_specs=(in_vmem, in_vmem, in_vmem),
        scratch_shapes=scratch,
        compiler_params=pltpu.CompilerParams(
            collective_id=0, has_side_effects=True, vmem_limit_bytes=56 * 1024 * 1024
        ),
        cost_estimate=pl.CostEstimate(flops=8_000_000_000, bytes_accessed=4_000_000, transcendentals=1_400_000),
    )(
        tokens.reshape(TH, TW, WID),
        out_grad.reshape(TH, TW, WID),
        qkv_weight.reshape(3, 4, WID, WID),
        out_weight,
    )
    d_tok, d_qkv, d_wo = pl.pallas_call(
        hand_out,
        out_shape=(
            jax.ShapeDtypeStruct((TH, TW, WID), BF16),
            jax.ShapeDtypeStruct((3, 16, WID), F32),
            jax.ShapeDtypeStruct((16, WID), F32),
        ),
        in_specs=[in_vmem] * 3,
        out_specs=(in_vmem, in_vmem, in_vmem),
    )(d_tok, d_qkv, d_wo)
    return d_tok.reshape(tokens.shape), d_qkv, d_wo.T


def solution(mesh):
    in_specs = (
        P("grid", None, None, "heads"),
        P(None, None, "heads"),
        P("heads", None),
        P("grid", None, None, "heads"),
    )
    out_specs = (P("grid", None, None, "heads"), P(None, "grid", "heads"), P("heads", "grid"))
    return jax.shard_map(local, mesh=mesh, in_specs=in_specs, out_specs=out_specs, check_vma=False)
```

```python
import jax
import jax.numpy as jnp
from jax import lax
from jax.experimental import pallas as pl
from jax.experimental.pallas import tpu as pltpu
from jax.sharding import PartitionSpec as P

MESH = pl.DeviceIdType.MESH
F32 = jnp.float32
BF16 = jnp.bfloat16

HD = 64
RAD = 6
LON = 8
LAT = 8
TH = 8
TW = 64
WID = 256
ROWS = TH * TW
EXT_R = TH + 2 * RAD
PAD = 8
EXT_C = TW + 2 * PAD
BW = 16
WINC = BW + 2 * PAD
KEYS = EXT_R * WINC
QN = TH * BW
NB = TW // BW
SLAB = RAD * BW
EDGE = TH * PAD
CORNER = RAD * PAD
PIECES = EXT_C // BW
ORDER = (0, 3, 1, 2)
BLOCKS = (1, 0, 3, 2)
DIRECT = 384


def mm(a, b, ca=1, cb=0):
    return lax.dot_general(a, b, (((ca,), (cb,)), ((), ())), preferred_element_type=F32)


def kernel(
    x_any, g_any, w_any, wo_any,
    tok_ref, dqkv_ref, dwo_ref,
    x_ref, g_ref, w_v, wo_v, xf, gf, kvb, edge, ns_r, ew_r, co_r, kvx, gx,
    q_s, do_s, o_s, dq_s, dkv, bias, xt, gt,
    gns_s, gew_s, gns_r, gew_r,
    e_s, e_r, l_s, l_r, own_e, own_l, pe_b, pl_b, e2_r, l2_r,
    m_s, m_f, m_r, own_m, pm_b, m2_r, own_3, e3_s, e3_r,
    tacc, t_s, t_r,
    w_sem, x_ss, x_rs, g_ss, g_rs, n_ss, n_rs, s_ss, s_rs, ew_ss, ew_rs, co_ss, co_rs,
    bn_ss, bn_rs, bs_ss, bs_rs, be_ss, be_rs,
    e_ss, e_rs, l_ss, l_rs, e2_ss, e2_rs, l2_ss, l2_rs, m_ss, m_rs, m2_ss, m2_rs, t_ss, t_rs, e3_sem,
):
    g = lax.axis_index("grid")
    h = lax.axis_index("heads")
    lat = lax.rem(g, LAT)
    lon = lax.div(g, LAT)
    sib = h + 1 - 2 * lax.rem(h, 2)
    far = h + 2 - 4 * lax.div(h, 2)
    opp = 3 - h
    slots = (h, sib, far, opp)

    x_load = pltpu.make_async_copy(x_any, x_ref, w_sem.at[2])
    g_load = pltpu.make_async_copy(g_any, g_ref, w_sem.at[3])
    w_copy = pltpu.make_async_copy(w_any, w_v, w_sem.at[0])
    wo_copy = pltpu.make_async_copy(wo_any, wo_v, w_sem.at[1])
    x_load.start()
    w_copy.start()
    g_load.start()
    wo_copy.start()

    def tile(dlat, dlon):
        return lax.rem(lon + dlon + LON, LON) * LAT + lax.rem(lat + dlat + LAT, LAT)

    has_n = lat > 0
    has_s = lat < LAT - 1
    can_send = (has_n, has_s)
    can_recv = (has_s, has_n)
    step = (-1, 1)

    bar = pltpu.get_barrier_semaphore()

    def greet(to_grid, to_head):
        pl.semaphore_signal(bar, inc=1, device_id=(to_grid, to_head), device_id_type=MESH)

    greet(g, sib)
    greet(g, far)
    for k in range(1, 8):
        greet(tile(k, 0), h)
        greet(tile(0, k), h)
    x_load.wait()
    pl.semaphore_wait(bar, 16)

    def rcopy(src, dst, ss, rs, to_grid, to_head):
        return pltpu.make_async_remote_copy(
            src_ref=src, dst_ref=dst, send_sem=ss, recv_sem=rs,
            device_id=(to_grid, to_head), device_id_type=MESH,
        )

    def gather(src, full, ss, rs, c):
        mine = src.at[:, c * BW : (c + 1) * BW, :]
        return (
            rcopy(mine, full.at[0, c], ss.at[c], rs.at[c], g, sib),
            rcopy(mine, full.at[1, c], ss.at[NB + c], rs.at[NB + c], g, far),
            rcopy(full.at[1, c], full.at[2, c], ss.at[2 * NB + c], rs.at[2 * NB + c], g, sib),
        )

    x_copies = [gather(x_ref, xf, x_ss, x_rs, c) for c in range(NB)]
    g_copies = [gather(g_ref, gf, g_ss, g_rs, c) for c in range(NB)]
    for c in ORDER:
        x_copies[c][1].start()
        x_copies[c][0].start()

    def chunk_of(ref, full, k, c):
        value = ref[:, c * BW : (c + 1) * BW, :] if k == 0 else full[k - 1, c]
        return value.reshape(QN, WID)

    key = lax.broadcasted_iota(jnp.int32, (KEYS, QN), 0)
    qry = lax.broadcasted_iota(jnp.int32, (KEYS, QN), 1)
    key_r, key_c = lax.div(key, WINC), lax.rem(key, WINC)
    dr = key_r - lax.div(qry, BW)
    dc = key_c - lax.rem(qry, BW)
    at_lat = key_r + (lat * TH - RAD)
    fine = (dr >= 0) & (dr <= 2 * RAD) & (dc >= PAD - RAD) & (dc <= PAD + RAD)
    fine = fine & (at_lat >= 0) & (at_lat < LAT * TH)
    bias[...] = jnp.where(fine, 0.0, -1e30)

    def clear(i, carry):
        gx[i] = jnp.zeros((EXT_C, 2 * WID), F32)
        return carry

    lax.fori_loop(0, EXT_R, clear, 0)
    body = slice(RAD, RAD + TH)
    rim = (slice(RAD + TH, EXT_R), slice(0, RAD))
    for way in range(2):

        def blank(way=way):
            kvx[rim[way], :, :] = jnp.zeros((RAD, EXT_C, 2 * WID), F32)

        pl.when(jnp.logical_not(can_recv[way]))(blank)
    w_copy.wait()
    g_load.wait()

    def ns_copy(way, c):
        rows = slice(0, SLAB) if way == 0 else slice(QN - SLAB, QN)
        ss, rs = (n_ss, n_rs) if way == 0 else (s_ss, s_rs)
        return rcopy(kvb.at[c, rows], ns_r.at[way, c], ss.at[c], rs.at[c], tile(step[way], 0), h)

    def ew_copy(way):
        return rcopy(edge.at[way], ew_r.at[way], ew_ss.at[way], ew_rs.at[way], tile(0, step[way]), h)

    def corner_copy(way, side):
        rows = slice(0, CORNER) if way == 0 else slice(EDGE - CORNER, EDGE)
        at = 2 * way + side
        return rcopy(ew_r.at[side, rows], co_r.at[at], co_ss.at[at], co_rs.at[at], tile(step[way], 0), h)

    def arrive(copies, c):
        copies[c][1].wait_recv()
        copies[c][2].start()

    for c in ORDER:
        total = [None, None]

        def add_kv(k, c=c, total=total):
            block = chunk_of(x_ref, xf, k, c)
            for i in range(2):
                part = mm(block, w_v[i + 1, slots[k]])
                total[i] = part if total[i] is None else total[i] + part

        add_kv(0)
        x_copies[c][0].wait_recv()
        add_kv(1)
        if c == ORDER[0]:
            arrive(x_copies, c)
        add_kv(2)
        if c != ORDER[-1]:
            arrive(x_copies, ORDER[ORDER.index(c) + 1])
        else:
            for other in BLOCKS:
                g_copies[other][1].start()
                g_copies[other][0].start()
        x_copies[c][2].wait_recv()
        add_kv(3)
        value = jnp.concatenate([total[0].astype(BF16), total[1].astype(BF16)], axis=1)
        kvb[c] = value
        for way in range(2):
            pl.when(can_send[way])(ns_copy(way, c).start)
        wide = value.astype(F32).reshape(TH, BW, 2 * WID)
        kvx[body, PAD + c * BW : PAD + (c + 1) * BW, :] = wide
        if c == 0:
            edge[0] = wide[:, :PAD, :].reshape(EDGE, 2 * WID).astype(BF16)
            ew_copy(0).start()
        if c == NB - 1:
            edge[1] = wide[:, BW - PAD :, :].reshape(EDGE, 2 * WID).astype(BF16)
            ew_copy(1).start()

    def turn(ref, full, out, c):
        for k in range(4):
            piece = chunk_of(ref, full, k, c)
            for j in range(2):
                part = piece[:, j * 128 : (j + 1) * 128].astype(F32)
                out[2 * slots[k] + j, :, c * QN : (c + 1) * QN] = part.T.astype(BF16)

    def query(c):
        total = mm(chunk_of(x_ref, xf, 0, c), w_v[0, slots[0]])
        for k in range(1, 4):
            total += mm(chunk_of(x_ref, xf, k, c), w_v[0, slots[k]])
        q_s[c] = total.astype(BF16) * jnp.asarray(HD**-0.5, BF16)

    def forward(side):
        ew_copy(side).wait_recv()
        for way in range(2):
            pl.when(can_send[way])(corner_copy(way, side).start)

    for c in ORDER:
        query(c)
    forward(0)
    for c in range(NB):
        turn(x_ref, xf, xt, c)
    forward(1)
    for side in range(2):
        cols = slice(PAD + TW, EXT_C) if side == 0 else slice(0, PAD)
        kvx[body, cols, :] = ew_r[side].astype(F32).reshape(TH, PAD, 2 * WID)

    wo_copy.wait()

    def cotangent(c, after):
        g_copies[c][0].wait_recv()
        total = None
        for k in range(4):
            if k == 3:
                if after is not None:
                    arrive(g_copies, after)
                g_copies[c][2].wait_recv()
            cols = pl.ds(pl.multiple_of(slots[k] * WID, WID), WID)
            part = mm(chunk_of(g_ref, gf, k, c), wo_v[:, cols], 1, 1)
            total = part if total is None else total + part
        do_s[c] = total.astype(BF16)
        turn(g_ref, gf, gt, c)

    def take_chunk(c):
        for way in range(2):

            def take(way=way):
                ns_copy(way, c).wait_recv()
                value = ns_r[way, c].astype(F32).reshape(RAD, BW, 2 * WID)
                kvx[rim[way], PAD + c * BW : PAD + (c + 1) * BW, :] = value

            pl.when(can_recv[way])(take)

    def take_corners(side):
        cols = slice(PAD + TW, EXT_C) if side == 0 else slice(0, PAD)
        for way in range(2):

            def take(way=way):
                corner_copy(way, side).wait_recv()
                kvx[rim[way], cols, :] = co_r[2 * way + side].astype(F32).reshape(RAD, PAD, 2 * WID)

            pl.when(can_recv[way])(take)

    lane = lax.broadcasted_iota(jnp.int32, (QN, 128), 1)
    first = lane < HD

    def two_heads(value):
        zero = jnp.zeros_like(value)
        return jnp.concatenate([jnp.where(first, value, zero), jnp.where(first, zero, value)], axis=0)

    def untwo(value):
        picked = jnp.concatenate([value[:HD, :QN], value[HD:, QN:]], axis=0)
        return picked.T.astype(BF16)

    def block(b):
        window = slice(b * BW, b * BW + WINC)
        for p in range(2):
            cols = slice(p * 128, (p + 1) * 128)
            vcols = slice(WID + p * 128, WID + (p + 1) * 128)
            keys = kvx[:, window, cols].reshape(KEYS, 128).astype(BF16)
            vals = kvx[:, window, vcols].reshape(KEYS, 128).astype(BF16)
            qq = two_heads(q_s[b, :, cols])
            dd = two_heads(do_s[b, :, cols])
            scores = mm(keys, qq, 1, 1)
            b1 = bias[...]
            raw = jnp.exp(scores + jnp.concatenate([b1, b1], axis=1))
            prob = raw * (1.0 / jnp.sum(raw, axis=0, keepdims=True))
            prob_b = prob.astype(BF16)
            d_prob = mm(vals, dd, 1, 1)
            delta = jnp.sum(prob * d_prob, axis=0, keepdims=True)
            d_sc = (prob * (d_prob - delta)).astype(BF16)
            o_s[b, :, cols] = untwo(mm(vals, prob_b, 0, 0))
            dq_s[b, :, cols] = untwo(mm(keys, d_sc, 0, 0) * HD**-0.5)
            gx[:, window, cols] += mm(d_sc, qq).reshape(EXT_R, WINC, 128)
            gx[:, window, vcols] += mm(prob_b, dd).reshape(EXT_R, WINC, 128)

    def back_copy(way, p):
        ss, rs = (bn_ss, bn_rs) if way == 0 else (bs_ss, bs_rs)
        return rcopy(gns_s.at[way, p], gns_r.at[way, p], ss.at[p], rs.at[p], tile(step[way], 0), h)

    def back_ew(way):
        return rcopy(gew_s.at[way], gew_r.at[way], be_ss.at[way], be_rs.at[way], tile(0, step[way]), h)

    def give(p):
        for way in range(2):
            rows = slice(0, RAD) if way == 0 else slice(RAD + TH, EXT_R)

            def send(way=way, rows=rows):
                value = gx[rows, p * BW : (p + 1) * BW, :].reshape(SLAB, 2 * WID)
                gns_s[way, p] = value.astype(BF16)
                back_copy(way, p).start()

            pl.when(can_send[way])(send)

    def fold(p):
        for way in range(2):
            rows = slice(TH, RAD + TH) if way == 0 else slice(RAD, 2 * RAD)

            def add(way=way, rows=rows):
                back_copy(way, p).wait_recv()
                value = gns_r[way, p].astype(F32).reshape(RAD, BW, 2 * WID)
                gx[rows, p * BW : (p + 1) * BW, :] += value

            pl.when(can_recv[way])(add)

    def give_ew(way):
        cols = slice(0, PAD) if way == 0 else slice(PAD + TW, EXT_C)
        gew_s[way] = gx[body, cols, :].reshape(EDGE, 2 * WID).astype(BF16)
        back_ew(way).start()

    def fold_ew(way):
        cols = slice(TW, TW + PAD) if way == 0 else slice(PAD, 2 * PAD)
        back_ew(way).wait_recv()
        gx[body, cols, :] += gew_r[way].astype(F32).reshape(TH, PAD, 2 * WID)

    arrive(g_copies, 1)
    cotangent(1, 0)
    for c in (0, 1, 2):
        take_chunk(c)
    block(1)
    cotangent(0, 3)
    take_corners(1)
    block(0)
    give(0)
    give(1)
    cotangent(3, 2)
    take_chunk(3)
    take_corners(0)
    block(3)
    give(4)
    cotangent(2, None)
    block(2)
    give(2)
    give(3)

    y_at = lax.div(lon, 2)
    x_at = lax.rem(lon, 2)

    def e_part(chunk):
        dq = dq_s[...].reshape(ROWS, WID)
        oo = o_s[...].reshape(ROWS, WID)
        return jnp.concatenate([mm(xt[chunk], dq), mm(gt[chunk], oo)], axis=1)

    e_plan = ((1, 0, 1), (1, 1, -1), (0, 1, 1), (2, 0, -1), (0, 0, 1), (2, 1, -1))

    def e_copy(k):
        at, half, to = e_plan[k]
        return rcopy(e_s.at[at, half], e_r.at[k], e_ss.at[k], e_rs.at[k], tile(0, 2 * to), h)

    def l_copy(k):
        return rcopy(l_s.at[k], l_r.at[k], l_ss.at[k], l_rs.at[k], tile(0, k + 1), h)

    def e_fill(at, half):
        to = lax.rem(y_at + at + 1, LON // 2)
        e_s[at, half] = e_part(2 * to + half).astype(BF16)

    for k in range(2):
        at, half, _ = e_plan[k]
        e_fill(at, half)
        e_copy(k).start()
    e_fill(0, 1)
    e_fill(2, 0)
    fold(0)
    give_ew(0)
    fold(4)
    give_ew(1)
    for k in range(2, 4):
        e_copy(k).start()
    e_fill(0, 0)
    e_fill(2, 1)
    for x in range(2):
        own_e[x] = e_part(2 * y_at + x)
    for k in range(2):
        e_copy(k).wait_recv()
        at, half, _ = e_plan[4 + k]
        e_s[at, half] = (e_s[at, half].astype(F32) + e_r[k].astype(F32)).astype(BF16)
        e_copy(4 + k).start()

    for s in range(4):
        tacc[s] = mm(dq_s[...].reshape(ROWS, WID), w_v[0, s], 1, 1)

    for p in (2, 1, 3):
        fold(p)
    for way in range(2):
        fold_ew(way)
    for c in range(NB):
        value = gx[body, PAD + c * BW : PAD + (c + 1) * BW, :].reshape(QN, 2 * WID)
        dkv[c * QN : (c + 1) * QN, :] = value.astype(BF16)

    def t_full(s):
        return (
            tacc[s]
            + mm(dkv[:, 0:WID], w_v[1, s], 1, 1)
            + mm(dkv[:, WID : 2 * WID], w_v[2, s], 1, 1)
        )

    t_opp = rcopy(t_s.at[0], t_r.at[0], t_ss.at[0], t_rs.at[0], g, sib)
    t_sib = rcopy(t_s.at[1], t_r.at[1], t_ss.at[1], t_rs.at[1], g, sib)
    t_far = rcopy(t_s.at[2], t_r.at[2], t_ss.at[2], t_rs.at[2], g, far)
    t_s[0] = t_full(opp).astype(BF16)
    t_opp.start()

    def m_copy(k):
        to = lax.rem(lat + k + 1, LAT)
        rows = pl.ds(pl.multiple_of(to * 16, 16), 16)
        return rcopy(m_s.at[:, rows], m_r.at[k], m_ss.at[k], m_rs.at[k], tile(k + 1, 0), h)

    def l_step(k, carry):
        l_s[k] = mm(xt[lax.rem(lon + k + 1, LON)], dkv[:, :DIRECT]).astype(BF16)
        l_copy(k).start()
        return carry

    def m_step(k, carry):
        full = mm(xt[k], dkv[:, DIRECT:])
        m_s[k] = full.astype(BF16)
        m_f[k] = full
        return carry

    lax.fori_loop(0, LON - 1, l_step, 0)
    lax.fori_loop(0, LON, m_step, 0)
    for k in range(LAT - 1):
        m_copy(k).start()
    own_l[...] = mm(xt[lon], dkv[:, :DIRECT])

    t_s[1] = t_full(sib).astype(BF16)
    t_sib.start()
    far_part = t_full(far)
    t_opp.wait_recv()
    t_s[2] = (far_part + t_r[0].astype(F32)).astype(BF16)
    t_far.start()
    tacc[h] = t_full(h)

    def e2_copy(k):
        to = lax.rem(lat + k + 1, LAT)
        rows = pl.ds(pl.multiple_of(to * 16, 16), 16)
        return rcopy(pe_b.at[:, rows], e2_r.at[k], e2_ss.at[k], e2_rs.at[k], tile(k + 1, 0), h)

    def l2_copy(k):
        to = lax.rem(lat + k + 1, LAT)
        rows = pl.ds(pl.multiple_of(to * 16, 16), 16)
        return rcopy(pl_b.at[rows], l2_r.at[k], l2_ss.at[k], l2_rs.at[k], tile(k + 1, 0), h)

    def level(own, first_copy, recv, packed, second_copy):
        def add(k, carry):
            first_copy(k).wait_recv()
            own[...] += recv[k].astype(F32)
            return carry

        lax.fori_loop(0, LON - 1, add, 0)
        packed[...] = own[...].astype(BF16)

        def send(k, carry):
            second_copy(k).start()
            return carry

        lax.fori_loop(0, LAT - 1, send, 0)

    def m2_copy(k):
        to = lax.rem(lon + k + 1, LON)
        return rcopy(pm_b.at[to], m2_r.at[k], m2_ss.at[k], m2_rs.at[k], tile(0, k + 1), h)

    for k in range(2, 6):
        e_copy(k).wait_recv()
        own_e[e_plan[k][1]] += e_r[k].astype(F32)
    pe_b[...] = own_e[...].astype(BF16)
    for k in range(LAT - 1):
        e2_copy(k).start()

    here = pl.ds(pl.multiple_of(lat * 16, 16), 16)
    total = m_f[:, here, :]
    for k in range(LAT - 1):
        m_copy(k).wait_recv()
        total += m_r[k].astype(F32)
    pm_b[...] = total.astype(BF16)
    own_m[...] = total
    for k in range(LON - 1):
        m2_copy(k).start()

    level(own_l, l_copy, l_r, pl_b, l2_copy)

    t_sib.wait_recv()
    t_far.wait_recv()
    for c in range(NB):
        rows = slice(c * QN, (c + 1) * QN)
        total = tacc[h, rows] + t_r[1, rows].astype(F32) + t_r[2, rows].astype(F32)
        tok_ref[:, c * BW : (c + 1) * BW, :] = total.astype(BF16).reshape(TH, BW, WID)

    def finish(own, second_copy, recv):
        total = own[here, :]
        for k in range(LAT - 1):
            second_copy(k).wait_recv()
            total += recv[k].astype(F32)
        return total

    early = own_e[:, here, :]
    for k in range(LAT - 1):
        e2_copy(k).wait_recv()
        early += e2_r[k].astype(F32)
    own_3[...] = early
    e3_s[...] = own_3[1 - x_at].astype(BF16)
    e3_copy = rcopy(e3_s, e3_r, e3_sem.at[0], e3_sem.at[1], tile(0, 1 - 2 * x_at), h)
    e3_copy.start()
    last = own_m[lon]
    for k in range(LON - 1):
        m2_copy(k).wait_recv()
        last += m2_r[k].astype(F32)
    late = jnp.concatenate([finish(own_l, l2_copy, l2_r), last], axis=1)
    dqkv_ref[1] = late[:, :WID]
    dqkv_ref[2] = late[:, WID:]
    e3_copy.wait_recv()
    early = own_3[x_at] + e3_r[...].astype(F32)
    dqkv_ref[0] = early[:, :WID]
    dwo_ref[...] = early[:, WID:]

    for copies in x_copies + g_copies + [(t_opp, t_sib, t_far, e3_copy)]:
        for copy in copies:
            copy.wait_send()
    for way in range(2):
        ew_copy(way).wait_send()
        back_ew(way).wait_send()

        def sent(way=way):
            for c in range(NB):
                ns_copy(way, c).wait_send()
            for side in range(2):
                corner_copy(way, side).wait_send()
            for p in range(PIECES):
                back_copy(way, p).wait_send()

        pl.when(can_send[way])(sent)

    for k in range(6):
        e_copy(k).wait_send()

    def drain(k, carry):
        l_copy(k).wait_send()
        e2_copy(k).wait_send()
        l2_copy(k).wait_send()
        m_copy(k).wait_send()
        m2_copy(k).wait_send()
        return carry

    lax.fori_loop(0, LON - 1, drain, 0)


def hand_out(tok_in, dqkv_in, dwo_in, tok_ref, dqkv_ref, dwo_ref):
    tok_ref[...] = tok_in[...]
    dqkv_ref[...] = dqkv_in[...]
    dwo_ref[...] = dwo_in[...]


def local(tokens, qkv_weight, out_weight, out_grad):
    vm = pltpu.VMEM
    dma = pltpu.SemaphoreType.DMA
    scratch = [
        vm((TH, TW, WID), BF16),
        vm((TH, TW, WID), BF16),
        vm((3, 4, WID, WID), BF16),
        vm((WID, 4 * WID), BF16),
        vm((3, NB, TH, BW, WID), BF16),
        vm((3, NB, TH, BW, WID), BF16),
        vm((NB, QN, 2 * WID), BF16),
        vm((2, EDGE, 2 * WID), BF16),
        vm((2, NB, SLAB, 2 * WID), BF16),
        vm((2, EDGE, 2 * WID), BF16),
        vm((4, CORNER, 2 * WID), BF16),
        vm((EXT_R, EXT_C, 2 * WID), F32),
        vm((EXT_R, EXT_C, 2 * WID), F32),
        vm((NB, QN, WID), BF16),
        vm((NB, QN, WID), BF16),
        vm((NB, QN, WID), BF16),
        vm((NB, QN, WID), BF16),
        vm((ROWS, 2 * WID), BF16),
        vm((KEYS, QN), F32),
        vm((LON, 128, ROWS), BF16),
        vm((LON, 128, ROWS), BF16),
        vm((2, PIECES, SLAB, 2 * WID), BF16),
        vm((2, EDGE, 2 * WID), BF16),
        vm((2, PIECES, SLAB, 2 * WID), BF16),
        vm((2, EDGE, 2 * WID), BF16),
        vm((LON // 2 - 1, 2, 128, 2 * WID), BF16),
        vm((6, 128, 2 * WID), BF16),
        vm((LON - 1, 128, DIRECT), BF16),
        vm((LON - 1, 128, DIRECT), BF16),
        vm((2, 128, 2 * WID), F32),
        vm((128, DIRECT), F32),
        vm((2, 128, 2 * WID), BF16),
        vm((128, DIRECT), BF16),
        vm((LAT - 1, 2, 16, 2 * WID), BF16),
        vm((LAT - 1, 16, DIRECT), BF16),
        vm((LON, 128, 2 * WID - DIRECT), BF16),
        vm((LON, 128, 2 * WID - DIRECT), F32),
        vm((LAT - 1, LON, 16, 2 * WID - DIRECT), BF16),
        vm((LON, 16, 2 * WID - DIRECT), F32),
        vm((LON, 16, 2 * WID - DIRECT), BF16),
        vm((LON - 1, 16, 2 * WID - DIRECT), BF16),
        vm((2, 16, 2 * WID), F32),
        vm((16, 2 * WID), BF16),
        vm((16, 2 * WID), BF16),
        vm((4, ROWS, WID), F32),
        vm((3, ROWS, WID), BF16),
        vm((3, ROWS, WID), BF16),
        dma((4,)),
        dma((3 * NB,)), dma((3 * NB,)),
        dma((3 * NB,)), dma((3 * NB,)),
        dma((NB,)), dma((NB,)),
        dma((NB,)), dma((NB,)),
        dma((2,)), dma((2,)),
        dma((4,)), dma((4,)),
        dma((PIECES,)), dma((PIECES,)),
        dma((PIECES,)), dma((PIECES,)),
        dma((2,)), dma((2,)),
        dma((7,)), dma((7,)),
        dma((7,)), dma((7,)),
        dma((7,)), dma((7,)),
        dma((7,)), dma((7,)),
        dma((7,)), dma((7,)),
        dma((7,)), dma((7,)),
        dma((3,)), dma((3,)),
        dma((2,)),
    ]
    in_vmem = pl.BlockSpec(memory_space=pltpu.VMEM)
    anywhere = pl.BlockSpec(memory_space=pl.ANY)
    d_tok, d_qkv, d_wo = pl.pallas_call(
        kernel,
        out_shape=(
            jax.ShapeDtypeStruct((TH, TW, WID), BF16),
            jax.ShapeDtypeStruct((3, 16, WID), F32),
            jax.ShapeDtypeStruct((16, WID), F32),
        ),
        in_specs=[anywhere] * 4,
        out_specs=(in_vmem, in_vmem, in_vmem),
        scratch_shapes=scratch,
        compiler_params=pltpu.CompilerParams(
            collective_id=0, has_side_effects=True, vmem_limit_bytes=56 * 1024 * 1024
        ),
        cost_estimate=pl.CostEstimate(flops=8_000_000_000, bytes_accessed=4_000_000, transcendentals=1_400_000),
    )(
        tokens.reshape(TH, TW, WID),
        out_grad.reshape(TH, TW, WID),
        qkv_weight.reshape(3, 4, WID, WID),
        out_weight,
    )
    d_tok, d_qkv, d_wo = pl.pallas_call(
        hand_out,
        out_shape=(
            jax.ShapeDtypeStruct((TH, TW, WID), BF16),
            jax.ShapeDtypeStruct((3, 16, WID), F32),
            jax.ShapeDtypeStruct((16, WID), F32),
        ),
        in_specs=[in_vmem] * 3,
        out_specs=(in_vmem, in_vmem, in_vmem),
    )(d_tok, d_qkv, d_wo)
    return d_tok.reshape(tokens.shape), d_qkv, d_wo.T


def solution(mesh):
    in_specs = (
        P("grid", None, None, "heads"),
        P(None, None, "heads"),
        P("heads", None),
        P("grid", None, None, "heads"),
    )
    out_specs = (P("grid", None, None, "heads"), P(None, "grid", "heads"), P("heads", "grid"))
    return jax.shard_map(local, mesh=mesh, in_specs=in_specs, out_specs=out_specs, check_vma=False)
```

```python
import jax
import jax.numpy as jnp
from jax import lax
from jax.experimental import pallas as pl
from jax.experimental.pallas import tpu as pltpu
from jax.sharding import PartitionSpec as P

MESH = pl.DeviceIdType.MESH
F32 = jnp.float32
BF16 = jnp.bfloat16

HD = 64
RAD = 6
LON = 8
LAT = 8
TH = 8
TW = 64
WID = 256
ROWS = TH * TW
EXT_R = TH + 2 * RAD
PAD = 8
EXT_C = TW + 2 * PAD
BW = 16
WINC = BW + 2 * PAD
KEYS = EXT_R * WINC
QN = TH * BW
NB = TW // BW
SLAB = RAD * BW
EDGE = TH * PAD
CORNER = RAD * PAD
PIECES = EXT_C // BW
ORDER = (0, 3, 1, 2)
BLOCKS = (1, 0, 3, 2)
DIRECT = 384


def mm(a, b, ca=1, cb=0):
    return lax.dot_general(a, b, (((ca,), (cb,)), ((), ())), preferred_element_type=F32)


def kernel(
    x_any, g_any, w_any, wo_any,
    tok_ref, dqkv_ref, dwo_ref,
    x_ref, g_ref, w_v, wo_v, xf, gf, kvb, edge, ns_r, ew_r, co_r, kvx, gx,
    q_s, do_s, o_s, dq_s, dkv, bias, xt, gt,
    gns_s, gew_s, gns_r, gew_r,
    e_s, e_r, l_s, l_r, own_e, own_l, pe_b, pl_b, e2_r, l2_r,
    m_s, m_f, m_r, own_m, pm_b, m2_r, own_3, e3_s, e3_r,
    tacc, t_s, t_r,
    w_sem, x_ss, x_rs, g_ss, g_rs, n_ss, n_rs, s_ss, s_rs, ew_ss, ew_rs, co_ss, co_rs,
    bn_ss, bn_rs, bs_ss, bs_rs, be_ss, be_rs,
    e_ss, e_rs, l_ss, l_rs, e2_ss, e2_rs, l2_ss, l2_rs, m_ss, m_rs, m2_ss, m2_rs, t_ss, t_rs, e3_sem,
):
    g = lax.axis_index("grid")
    h = lax.axis_index("heads")
    lat = lax.rem(g, LAT)
    lon = lax.div(g, LAT)
    sib = h + 1 - 2 * lax.rem(h, 2)
    far = h + 2 - 4 * lax.div(h, 2)
    opp = 3 - h
    slots = (h, sib, far, opp)

    x_load = pltpu.make_async_copy(x_any, x_ref, w_sem.at[2])
    g_load = pltpu.make_async_copy(g_any, g_ref, w_sem.at[3])
    w_copy = pltpu.make_async_copy(w_any, w_v, w_sem.at[0])
    wo_copy = pltpu.make_async_copy(wo_any, wo_v, w_sem.at[1])
    x_load.start()
    w_copy.start()
    g_load.start()
    wo_copy.start()

    def tile(dlat, dlon):
        return lax.rem(lon + dlon + LON, LON) * LAT + lax.rem(lat + dlat + LAT, LAT)

    has_n = lat > 0
    has_s = lat < LAT - 1
    can_send = (has_n, has_s)
    can_recv = (has_s, has_n)
    step = (-1, 1)

    bar = pltpu.get_barrier_semaphore()

    def greet(to_grid, to_head):
        pl.semaphore_signal(bar, inc=1, device_id=(to_grid, to_head), device_id_type=MESH)

    greet(g, sib)
    greet(g, far)
    for k in range(1, 8):
        greet(tile(k, 0), h)
        greet(tile(0, k), h)
    x_load.wait()
    pl.semaphore_wait(bar, 16)

    def rcopy(src, dst, ss, rs, to_grid, to_head):
        return pltpu.make_async_remote_copy(
            src_ref=src, dst_ref=dst, send_sem=ss, recv_sem=rs,
            device_id=(to_grid, to_head), device_id_type=MESH,
        )

    def gather(src, full, ss, rs, c):
        mine = src.at[:, c * BW : (c + 1) * BW, :]
        return (
            rcopy(mine, full.at[0, c], ss.at[c], rs.at[c], g, sib),
            rcopy(mine, full.at[1, c], ss.at[NB + c], rs.at[NB + c], g, far),
            rcopy(full.at[1, c], full.at[2, c], ss.at[2 * NB + c], rs.at[2 * NB + c], g, sib),
        )

    x_copies = [gather(x_ref, xf, x_ss, x_rs, c) for c in range(NB)]
    g_copies = [gather(g_ref, gf, g_ss, g_rs, c) for c in range(NB)]
    for c in ORDER:
        x_copies[c][1].start()
        x_copies[c][0].start()

    def chunk_of(ref, full, k, c):
        value = ref[:, c * BW : (c + 1) * BW, :] if k == 0 else full[k - 1, c]
        return value.reshape(QN, WID)

    key = lax.broadcasted_iota(jnp.int32, (KEYS, QN), 0)
    qry = lax.broadcasted_iota(jnp.int32, (KEYS, QN), 1)
    key_r, key_c = lax.div(key, WINC), lax.rem(key, WINC)
    dr = key_r - lax.div(qry, BW)
    dc = key_c - lax.rem(qry, BW)
    at_lat = key_r + (lat * TH - RAD)
    fine = (dr >= 0) & (dr <= 2 * RAD) & (dc >= PAD - RAD) & (dc <= PAD + RAD)
    fine = fine & (at_lat >= 0) & (at_lat < LAT * TH)
    bias[...] = jnp.where(fine, 0.0, -1e30)

    def clear(i, carry):
        gx[i] = jnp.zeros((EXT_C, 2 * WID), F32)
        return carry

    lax.fori_loop(0, EXT_R, clear, 0)
    body = slice(RAD, RAD + TH)
    rim = (slice(RAD + TH, EXT_R), slice(0, RAD))
    for way in range(2):

        def blank(way=way):
            kvx[rim[way], :, :] = jnp.zeros((RAD, EXT_C, 2 * WID), F32)

        pl.when(jnp.logical_not(can_recv[way]))(blank)
    w_copy.wait()
    g_load.wait()

    def ns_copy(way, c):
        rows = slice(0, SLAB) if way == 0 else slice(QN - SLAB, QN)
        ss, rs = (n_ss, n_rs) if way == 0 else (s_ss, s_rs)
        return rcopy(kvb.at[c, rows], ns_r.at[way, c], ss.at[c], rs.at[c], tile(step[way], 0), h)

    def ew_copy(way):
        return rcopy(edge.at[way], ew_r.at[way], ew_ss.at[way], ew_rs.at[way], tile(0, step[way]), h)

    def corner_copy(way, side):
        rows = slice(0, CORNER) if way == 0 else slice(EDGE - CORNER, EDGE)
        at = 2 * way + side
        return rcopy(ew_r.at[side, rows], co_r.at[at], co_ss.at[at], co_rs.at[at], tile(step[way], 0), h)

    def arrive(copies, c):
        copies[c][1].wait_recv()
        copies[c][2].start()

    for c in ORDER:
        total = [None, None]

        def add_kv(k, c=c, total=total):
            block = chunk_of(x_ref, xf, k, c)
            for i in range(2):
                part = mm(block, w_v[i + 1, slots[k]])
                total[i] = part if total[i] is None else total[i] + part

        add_kv(0)
        x_copies[c][0].wait_recv()
        add_kv(1)
        if c == ORDER[0]:
            arrive(x_copies, c)
        add_kv(2)
        if c != ORDER[-1]:
            arrive(x_copies, ORDER[ORDER.index(c) + 1])
        else:
            for other in BLOCKS:
                g_copies[other][1].start()
                g_copies[other][0].start()
        x_copies[c][2].wait_recv()
        add_kv(3)
        value = jnp.concatenate([total[0].astype(BF16), total[1].astype(BF16)], axis=1)
        kvb[c] = value
        for way in range(2):
            pl.when(can_send[way])(ns_copy(way, c).start)
        wide = value.astype(F32).reshape(TH, BW, 2 * WID)
        kvx[body, PAD + c * BW : PAD + (c + 1) * BW, :] = wide
        if c == 0:
            edge[0] = wide[:, :PAD, :].reshape(EDGE, 2 * WID).astype(BF16)
            ew_copy(0).start()
        if c == NB - 1:
            edge[1] = wide[:, BW - PAD :, :].reshape(EDGE, 2 * WID).astype(BF16)
            ew_copy(1).start()

    def turn(ref, full, out, c):
        for k in range(4):
            piece = chunk_of(ref, full, k, c)
            for j in range(2):
                part = piece[:, j * 128 : (j + 1) * 128].astype(F32)
                out[2 * slots[k] + j, :, c * QN : (c + 1) * QN] = part.T.astype(BF16)

    def query(c):
        total = mm(chunk_of(x_ref, xf, 0, c), w_v[0, slots[0]])
        for k in range(1, 4):
            total += mm(chunk_of(x_ref, xf, k, c), w_v[0, slots[k]])
        q_s[c] = total.astype(BF16) * jnp.asarray(HD**-0.5, BF16)

    def forward(side):
        ew_copy(side).wait_recv()
        for way in range(2):
            pl.when(can_send[way])(corner_copy(way, side).start)

    for c in ORDER:
        query(c)
    forward(0)
    for c in range(NB):
        turn(x_ref, xf, xt, c)
    forward(1)
    for side in range(2):
        cols = slice(PAD + TW, EXT_C) if side == 0 else slice(0, PAD)
        kvx[body, cols, :] = ew_r[side].astype(F32).reshape(TH, PAD, 2 * WID)

    wo_copy.wait()

    def cotangent(c, after):
        g_copies[c][0].wait_recv()
        total = None
        for k in range(4):
            if k == 3:
                if after is not None:
                    arrive(g_copies, after)
                g_copies[c][2].wait_recv()
            cols = pl.ds(pl.multiple_of(slots[k] * WID, WID), WID)
            part = mm(chunk_of(g_ref, gf, k, c), wo_v[:, cols], 1, 1)
            total = part if total is None else total + part
        do_s[c] = total.astype(BF16)
        turn(g_ref, gf, gt, c)

    def take_chunk(c):
        for way in range(2):

            def take(way=way):
                ns_copy(way, c).wait_recv()
                value = ns_r[way, c].astype(F32).reshape(RAD, BW, 2 * WID)
                kvx[rim[way], PAD + c * BW : PAD + (c + 1) * BW, :] = value

            pl.when(can_recv[way])(take)

    def take_corners(side):
        cols = slice(PAD + TW, EXT_C) if side == 0 else slice(0, PAD)
        for way in range(2):

            def take(way=way):
                corner_copy(way, side).wait_recv()
                kvx[rim[way], cols, :] = co_r[2 * way + side].astype(F32).reshape(RAD, PAD, 2 * WID)

            pl.when(can_recv[way])(take)

    lane = lax.broadcasted_iota(jnp.int32, (QN, 128), 1)
    first = lane < HD

    def two_heads(value):
        zero = jnp.zeros_like(value)
        return jnp.concatenate([jnp.where(first, value, zero), jnp.where(first, zero, value)], axis=0)

    def untwo(value):
        picked = jnp.concatenate([value[:HD, :QN], value[HD:, QN:]], axis=0)
        return picked.T.astype(BF16)

    def block(b):
        window = slice(b * BW, b * BW + WINC)
        for p in range(2):
            cols = slice(p * 128, (p + 1) * 128)
            vcols = slice(WID + p * 128, WID + (p + 1) * 128)
            keys = kvx[:, window, cols].reshape(KEYS, 128).astype(BF16)
            vals = kvx[:, window, vcols].reshape(KEYS, 128).astype(BF16)
            qq = two_heads(q_s[b, :, cols])
            dd = two_heads(do_s[b, :, cols])
            scores = mm(keys, qq, 1, 1)
            b1 = bias[...]
            raw = jnp.exp(scores + jnp.concatenate([b1, b1], axis=1))
            prob = raw * (1.0 / jnp.sum(raw, axis=0, keepdims=True))
            prob_b = prob.astype(BF16)
            d_prob = mm(vals, dd, 1, 1)
            delta = jnp.sum(prob * d_prob, axis=0, keepdims=True)
            d_sc = (prob * (d_prob - delta)).astype(BF16)
            o_s[b, :, cols] = untwo(mm(vals, prob_b, 0, 0))
            dq_s[b, :, cols] = untwo(mm(keys, d_sc, 0, 0) * HD**-0.5)
            gx[:, window, cols] += mm(d_sc, qq).reshape(EXT_R, WINC, 128)
            gx[:, window, vcols] += mm(prob_b, dd).reshape(EXT_R, WINC, 128)

    def back_copy(way, p):
        ss, rs = (bn_ss, bn_rs) if way == 0 else (bs_ss, bs_rs)
        return rcopy(gns_s.at[way, p], gns_r.at[way, p], ss.at[p], rs.at[p], tile(step[way], 0), h)

    def back_ew(way):
        return rcopy(gew_s.at[way], gew_r.at[way], be_ss.at[way], be_rs.at[way], tile(0, step[way]), h)

    def give(p):
        for way in range(2):
            rows = slice(0, RAD) if way == 0 else slice(RAD + TH, EXT_R)

            def send(way=way, rows=rows):
                value = gx[rows, p * BW : (p + 1) * BW, :].reshape(SLAB, 2 * WID)
                gns_s[way, p] = value.astype(BF16)
                back_copy(way, p).start()

            pl.when(can_send[way])(send)

    def fold(p):
        for way in range(2):
            rows = slice(TH, RAD + TH) if way == 0 else slice(RAD, 2 * RAD)

            def add(way=way, rows=rows):
                back_copy(way, p).wait_recv()
                value = gns_r[way, p].astype(F32).reshape(RAD, BW, 2 * WID)
                gx[rows, p * BW : (p + 1) * BW, :] += value

            pl.when(can_recv[way])(add)

    def give_ew(way):
        cols = slice(0, PAD) if way == 0 else slice(PAD + TW, EXT_C)
        gew_s[way] = gx[body, cols, :].reshape(EDGE, 2 * WID).astype(BF16)
        back_ew(way).start()

    def fold_ew(way):
        cols = slice(TW, TW + PAD) if way == 0 else slice(PAD, 2 * PAD)
        back_ew(way).wait_recv()
        gx[body, cols, :] += gew_r[way].astype(F32).reshape(TH, PAD, 2 * WID)

    arrive(g_copies, 1)
    cotangent(1, 0)
    for c in (0, 1, 2):
        take_chunk(c)
    block(1)
    cotangent(0, 3)
    take_corners(1)
    block(0)
    give(0)
    give(1)
    cotangent(3, 2)
    take_chunk(3)
    take_corners(0)
    block(3)
    give(4)
    cotangent(2, None)
    block(2)
    give(2)
    give(3)

    y_at = lax.div(lon, 2)
    x_at = lax.rem(lon, 2)

    def e_part(chunk):
        dq = dq_s[...].reshape(ROWS, WID)
        oo = o_s[...].reshape(ROWS, WID)
        return jnp.concatenate([mm(xt[chunk], dq), mm(gt[chunk], oo)], axis=1)

    e_plan = ((1, 0, 1), (1, 1, -1), (0, 1, 1), (2, 0, -1), (0, 0, 1), (2, 1, -1))

    def e_copy(k):
        at, half, to = e_plan[k]
        return rcopy(e_s.at[at, half], e_r.at[k], e_ss.at[k], e_rs.at[k], tile(0, 2 * to), h)

    def l_copy(k):
        return rcopy(l_s.at[k], l_r.at[k], l_ss.at[k], l_rs.at[k], tile(0, k + 1), h)

    def e_fill(at, half):
        to = lax.rem(y_at + at + 1, LON // 2)
        e_s[at, half] = e_part(2 * to + half).astype(BF16)

    for k in range(2):
        at, half, _ = e_plan[k]
        e_fill(at, half)
        e_copy(k).start()
    e_fill(0, 1)
    e_fill(2, 0)
    fold(0)
    give_ew(0)
    fold(4)
    give_ew(1)
    for k in range(2, 4):
        e_copy(k).start()
    e_fill(0, 0)
    e_fill(2, 1)
    for x in range(2):
        own_e[x] = e_part(2 * y_at + x)
    for k in range(2):
        e_copy(k).wait_recv()
        at, half, _ = e_plan[4 + k]
        e_s[at, half] = (e_s[at, half].astype(F32) + e_r[k].astype(F32)).astype(BF16)
        e_copy(4 + k).start()

    for s in range(4):
        tacc[s] = mm(dq_s[...].reshape(ROWS, WID), w_v[0, s], 1, 1)

    for p in (2, 1, 3):
        fold(p)
    for way in range(2):
        fold_ew(way)
    for c in range(NB):
        value = gx[body, PAD + c * BW : PAD + (c + 1) * BW, :].reshape(QN, 2 * WID)
        dkv[c * QN : (c + 1) * QN, :] = value.astype(BF16)

    def t_full(s):
        return (
            tacc[s]
            + mm(dkv[:, 0:WID], w_v[1, s], 1, 1)
            + mm(dkv[:, WID : 2 * WID], w_v[2, s], 1, 1)
        )

    t_opp = rcopy(t_s.at[0], t_r.at[0], t_ss.at[0], t_rs.at[0], g, sib)
    t_sib = rcopy(t_s.at[1], t_r.at[1], t_ss.at[1], t_rs.at[1], g, sib)
    t_far = rcopy(t_s.at[2], t_r.at[2], t_ss.at[2], t_rs.at[2], g, far)
    t_s[0] = t_full(opp).astype(BF16)
    t_opp.start()

    def m_copy(k):
        to = lax.rem(lat + k + 1, LAT)
        rows = pl.ds(pl.multiple_of(to * 16, 16), 16)
        return rcopy(m_s.at[:, rows], m_r.at[k], m_ss.at[k], m_rs.at[k], tile(k + 1, 0), h)

    def l_step(k, carry):
        l_s[k] = mm(xt[lax.rem(lon + k + 1, LON)], dkv[:, :DIRECT]).astype(BF16)
        l_copy(k).start()
        return carry

    def m_step(k, carry):
        full = mm(xt[k], dkv[:, DIRECT:])
        m_s[k] = full.astype(BF16)
        m_f[k] = full
        return carry

    lax.fori_loop(0, LON, m_step, 0)
    for k in range(LAT - 1):
        m_copy(k).start()
    lax.fori_loop(0, LON - 1, l_step, 0)
    own_l[...] = mm(xt[lon], dkv[:, :DIRECT])

    t_s[1] = t_full(sib).astype(BF16)
    t_sib.start()
    far_part = t_full(far)
    t_opp.wait_recv()
    t_s[2] = (far_part + t_r[0].astype(F32)).astype(BF16)
    t_far.start()
    tacc[h] = t_full(h)

    def e2_copy(k):
        to = lax.rem(lat + k + 1, LAT)
        rows = pl.ds(pl.multiple_of(to * 16, 16), 16)
        return rcopy(pe_b.at[:, rows], e2_r.at[k], e2_ss.at[k], e2_rs.at[k], tile(k + 1, 0), h)

    def l2_copy(k):
        to = lax.rem(lat + k + 1, LAT)
        rows = pl.ds(pl.multiple_of(to * 16, 16), 16)
        return rcopy(pl_b.at[rows], l2_r.at[k], l2_ss.at[k], l2_rs.at[k], tile(k + 1, 0), h)

    def level(own, first_copy, recv, packed, second_copy):
        def add(k, carry):
            first_copy(k).wait_recv()
            own[...] += recv[k].astype(F32)
            return carry

        lax.fori_loop(0, LON - 1, add, 0)
        packed[...] = own[...].astype(BF16)

        def send(k, carry):
            second_copy(k).start()
            return carry

        lax.fori_loop(0, LAT - 1, send, 0)

    def m2_copy(k):
        to = lax.rem(lon + k + 1, LON)
        return rcopy(pm_b.at[to], m2_r.at[k], m2_ss.at[k], m2_rs.at[k], tile(0, k + 1), h)

    for k in range(2, 6):
        e_copy(k).wait_recv()
        own_e[e_plan[k][1]] += e_r[k].astype(F32)
    pe_b[...] = own_e[...].astype(BF16)
    for k in range(LAT - 1):
        e2_copy(k).start()

    here = pl.ds(pl.multiple_of(lat * 16, 16), 16)
    total = m_f[:, here, :]
    for k in range(LAT - 1):
        m_copy(k).wait_recv()
        total += m_r[k].astype(F32)
    pm_b[...] = total.astype(BF16)
    own_m[...] = total
    for k in range(LON - 1):
        m2_copy(k).start()

    level(own_l, l_copy, l_r, pl_b, l2_copy)

    t_sib.wait_recv()
    t_far.wait_recv()
    for c in range(NB):
        rows = slice(c * QN, (c + 1) * QN)
        total = tacc[h, rows] + t_r[1, rows].astype(F32) + t_r[2, rows].astype(F32)
        tok_ref[:, c * BW : (c + 1) * BW, :] = total.astype(BF16).reshape(TH, BW, WID)

    def finish(own, second_copy, recv):
        total = own[here, :]
        for k in range(LAT - 1):
            second_copy(k).wait_recv()
            total += recv[k].astype(F32)
        return total

    early = own_e[:, here, :]
    for k in range(LAT - 1):
        e2_copy(k).wait_recv()
        early += e2_r[k].astype(F32)
    own_3[...] = early
    e3_s[...] = own_3[1 - x_at].astype(BF16)
    e3_copy = rcopy(e3_s, e3_r, e3_sem.at[0], e3_sem.at[1], tile(0, 1 - 2 * x_at), h)
    e3_copy.start()
    last = own_m[lon]
    for k in range(LON - 1):
        m2_copy(k).wait_recv()
        last += m2_r[k].astype(F32)
    late = jnp.concatenate([finish(own_l, l2_copy, l2_r), last], axis=1)
    dqkv_ref[1] = late[:, :WID]
    dqkv_ref[2] = late[:, WID:]
    e3_copy.wait_recv()
    early = own_3[x_at] + e3_r[...].astype(F32)
    dqkv_ref[0] = early[:, :WID]
    dwo_ref[...] = early[:, WID:]

    for copies in x_copies + g_copies + [(t_opp, t_sib, t_far, e3_copy)]:
        for copy in copies:
            copy.wait_send()
    for way in range(2):
        ew_copy(way).wait_send()
        back_ew(way).wait_send()

        def sent(way=way):
            for c in range(NB):
                ns_copy(way, c).wait_send()
            for side in range(2):
                corner_copy(way, side).wait_send()
            for p in range(PIECES):
                back_copy(way, p).wait_send()

        pl.when(can_send[way])(sent)

    for k in range(6):
        e_copy(k).wait_send()

    def drain(k, carry):
        l_copy(k).wait_send()
        e2_copy(k).wait_send()
        l2_copy(k).wait_send()
        m_copy(k).wait_send()
        m2_copy(k).wait_send()
        return carry

    lax.fori_loop(0, LON - 1, drain, 0)


def hand_out(tok_in, dqkv_in, dwo_in, tok_ref, dqkv_ref, dwo_ref):
    tok_ref[...] = tok_in[...]
    dqkv_ref[...] = dqkv_in[...]
    dwo_ref[...] = dwo_in[...]


def local(tokens, qkv_weight, out_weight, out_grad):
    vm = pltpu.VMEM
    dma = pltpu.SemaphoreType.DMA
    scratch = [
        vm((TH, TW, WID), BF16),
        vm((TH, TW, WID), BF16),
        vm((3, 4, WID, WID), BF16),
        vm((WID, 4 * WID), BF16),
        vm((3, NB, TH, BW, WID), BF16),
        vm((3, NB, TH, BW, WID), BF16),
        vm((NB, QN, 2 * WID), BF16),
        vm((2, EDGE, 2 * WID), BF16),
        vm((2, NB, SLAB, 2 * WID), BF16),
        vm((2, EDGE, 2 * WID), BF16),
        vm((4, CORNER, 2 * WID), BF16),
        vm((EXT_R, EXT_C, 2 * WID), F32),
        vm((EXT_R, EXT_C, 2 * WID), F32),
        vm((NB, QN, WID), BF16),
        vm((NB, QN, WID), BF16),
        vm((NB, QN, WID), BF16),
        vm((NB, QN, WID), BF16),
        vm((ROWS, 2 * WID), BF16),
        vm((KEYS, QN), F32),
        vm((LON, 128, ROWS), BF16),
        vm((LON, 128, ROWS), BF16),
        vm((2, PIECES, SLAB, 2 * WID), BF16),
        vm((2, EDGE, 2 * WID), BF16),
        vm((2, PIECES, SLAB, 2 * WID), BF16),
        vm((2, EDGE, 2 * WID), BF16),
        vm((LON // 2 - 1, 2, 128, 2 * WID), BF16),
        vm((6, 128, 2 * WID), BF16),
        vm((LON - 1, 128, DIRECT), BF16),
        vm((LON - 1, 128, DIRECT), BF16),
        vm((2, 128, 2 * WID), F32),
        vm((128, DIRECT), F32),
        vm((2, 128, 2 * WID), BF16),
        vm((128, DIRECT), BF16),
        vm((LAT - 1, 2, 16, 2 * WID), BF16),
        vm((LAT - 1, 16, DIRECT), BF16),
        vm((LON, 128, 2 * WID - DIRECT), BF16),
        vm((LON, 128, 2 * WID - DIRECT), F32),
        vm((LAT - 1, LON, 16, 2 * WID - DIRECT), BF16),
        vm((LON, 16, 2 * WID - DIRECT), F32),
        vm((LON, 16, 2 * WID - DIRECT), BF16),
        vm((LON - 1, 16, 2 * WID - DIRECT), BF16),
        vm((2, 16, 2 * WID), F32),
        vm((16, 2 * WID), BF16),
        vm((16, 2 * WID), BF16),
        vm((4, ROWS, WID), F32),
        vm((3, ROWS, WID), BF16),
        vm((3, ROWS, WID), BF16),
        dma((4,)),
        dma((3 * NB,)), dma((3 * NB,)),
        dma((3 * NB,)), dma((3 * NB,)),
        dma((NB,)), dma((NB,)),
        dma((NB,)), dma((NB,)),
        dma((2,)), dma((2,)),
        dma((4,)), dma((4,)),
        dma((PIECES,)), dma((PIECES,)),
        dma((PIECES,)), dma((PIECES,)),
        dma((2,)), dma((2,)),
        dma((7,)), dma((7,)),
        dma((7,)), dma((7,)),
        dma((7,)), dma((7,)),
        dma((7,)), dma((7,)),
        dma((7,)), dma((7,)),
        dma((7,)), dma((7,)),
        dma((3,)), dma((3,)),
        dma((2,)),
    ]
    in_vmem = pl.BlockSpec(memory_space=pltpu.VMEM)
    anywhere = pl.BlockSpec(memory_space=pl.ANY)
    d_tok, d_qkv, d_wo = pl.pallas_call(
        kernel,
        out_shape=(
            jax.ShapeDtypeStruct((TH, TW, WID), BF16),
            jax.ShapeDtypeStruct((3, 16, WID), F32),
            jax.ShapeDtypeStruct((16, WID), F32),
        ),
        in_specs=[anywhere] * 4,
        out_specs=(in_vmem, in_vmem, in_vmem),
        scratch_shapes=scratch,
        compiler_params=pltpu.CompilerParams(
            collective_id=0, has_side_effects=True, vmem_limit_bytes=56 * 1024 * 1024
        ),
        cost_estimate=pl.CostEstimate(flops=8_000_000_000, bytes_accessed=4_000_000, transcendentals=1_400_000),
    )(
        tokens.reshape(TH, TW, WID),
        out_grad.reshape(TH, TW, WID),
        qkv_weight.reshape(3, 4, WID, WID),
        out_weight,
    )
    d_tok, d_qkv, d_wo = pl.pallas_call(
        hand_out,
        out_shape=(
            jax.ShapeDtypeStruct((TH, TW, WID), BF16),
            jax.ShapeDtypeStruct((3, 16, WID), F32),
            jax.ShapeDtypeStruct((16, WID), F32),
        ),
        in_specs=[in_vmem] * 3,
        out_specs=(in_vmem, in_vmem, in_vmem),
    )(d_tok, d_qkv, d_wo)
    return d_tok.reshape(tokens.shape), d_qkv, d_wo.T


def solution(mesh):
    in_specs = (
        P("grid", None, None, "heads"),
        P(None, None, "heads"),
        P("heads", None),
        P("grid", None, None, "heads"),
    )
    out_specs = (P("grid", None, None, "heads"), P(None, "grid", "heads"), P("heads", "grid"))
    return jax.shard_map(local, mesh=mesh, in_specs=in_specs, out_specs=out_specs, check_vma=False)
```
